32 devices in a mesh: phi: 8 (over z, core), mom: 4 (over y, x).
Axes of the slice: x: 2, y: 2, z: 4, core: 2. Of those that a mesh axis runs over, the one named last changes fastest.
Arguments:
- spectra: float32 [32, 4, 16, 64, 256], P('mom', None, 'phi'), may hold values from 0.1 to 3
- production: bfloat16 [32, 32], replicated, may hold values from 0 to 0.119628906
- bin_group: int32 [32], replicated, may hold values from 0 to 3
- parent_of: int32 [4], replicated, may hold values from 0 to 3
- diffusivity: float32 [64, 256], replicated, may hold values from 0.05 to 0.22
- height_inverse: float32 [64, 64], replicated, may hold values from -1 to 1, as said below
- loss_rate: float32 [32], P('mom'), may hold values from 2 to 20
- density: float32 [16, 64, 256], P('phi'), may hold values from 0.5 to 2
Outputs:
- spectra_out: float32 [32, 4, 16, 64, 256], P('mom', None, 'phi')
The draws below stay inside these ranges and needn't reach their ends.
Inputs may be any that keep to these rules, and one draw needn't show every extreme that they name: `height_inverse`: diagonal entries lie between 0.7 and 1, off-diagonal entries are small.
All inputs are finite; a program needn't handle non-finite values.
Results may differ from the reference program's by a relative error of at most 0.00085.
Values may be sent and summed in bfloat16 or wider, within the bound.
A program may use at most 64 MiB of HBM per device.

```python
import math
import jax
import jax.numpy as jnp
from jax import lax

P_SIZE = 32
S = 4
Z = 64
R = 256
STEPS = 1
NPHI = 16


def draw_height_inverse(key, part):
    first, second = jax.random.split(jax.random.fold_in(key, 17))
    diagonal = jax.random.uniform(first, (Z,), jnp.float32, 0.7, 1.0)
    spread = jnp.clip(jax.random.normal(second, (Z, Z), jnp.float32), -4.0, 4.0)
    eye_mask = jnp.eye(Z, dtype=jnp.float32)
    off_part = spread * (0.1 / jnp.sqrt(jnp.float32(Z))) * (1.0 - eye_mask)
    return eye_mask * diagonal[None, :] + off_part


def with_ends(values, own_key, low, top_value):
    extent = values.shape
    index_at = [jax.random.randint(jax.random.fold_in(own_key, axis), (), 0, extent[axis]) for axis in range(len(extent))]
    values = values.at[tuple(index_at)].set(low)
    longest = extent.index(max(extent))
    index_at[longest] = (index_at[longest] + 1) % extent[longest]
    return values.at[tuple(index_at)].set(top_value)


def block_levels(key, dims, cuts, low, high):
    def one(position, blocks):
        steps = jax.random.uniform(jax.random.fold_in(jax.random.fold_in(key, 6), position), (blocks,), jnp.float32, low / len(cuts), high / len(cuts))
        return jnp.repeat(jnp.exp(steps), dims[position] // blocks).reshape((-1,) + (1,) * (len(dims) - position - 1))

    loudness = one(*cuts[0])
    for cut in cuts[1:]:
        loudness = loudness * one(*cut)
    return loudness


def setup_inputs(seed: int = 0) -> dict:
    seeds = jax.random.split(jax.random.key(seed), 9)
    return {
        "spectra": jnp.clip(jnp.exp(math.log(3.0) - 3.4011974 * jax.random.uniform(seeds[0], (P_SIZE, S, NPHI, Z, R), jnp.float32) ** block_levels(seeds[0], (P_SIZE, S, NPHI, Z, R), ((0, 4), (2, 8)), -0.2, 0.2)), 0.1, 3.0),
        "production": jnp.clip(jax.random.uniform(seeds[1], (P_SIZE, P_SIZE), jnp.float32, 0.0, 0.119628906), 0.0, 0.119628906).astype(jnp.bfloat16),
        "bin_group": with_ends(jax.random.randint(seeds[2], (P_SIZE,), 0, 4), jax.random.fold_in(seeds[2], 1), 0, 3).astype(jnp.int32),
        "parent_of": with_ends(jax.random.randint(seeds[3], (S,), 0, S), jax.random.fold_in(seeds[3], 1), 0, S - 1).astype(jnp.int32),
        "diffusivity": jnp.clip(jnp.exp(jax.random.uniform(seeds[4], (Z, R), jnp.float32, math.log(0.05), math.log(0.22))), 0.05, 0.22),
        "height_inverse": draw_height_inverse(jax.random.fold_in(seeds[8], 71), 0),
        "loss_rate": jnp.clip(jnp.exp(math.log(20.0) - 2.3025851 * jax.random.uniform(seeds[6], (P_SIZE,), jnp.float32) ** block_levels(seeds[6], (P_SIZE,), ((0, 4),), -0.2, 0.2)), 2.0, 20.0),
        "density": jnp.clip(0.5 + 1.5 * jax.random.uniform(seeds[7], (NPHI, Z, R), jnp.float32) ** block_levels(seeds[7], (NPHI, Z, R), ((0, 8),), -0.2, 0.2), 0.5, 2.0),
    }


def one_step(state, production, bin_group, parent_of, diffusivity, height_inverse, loss_rate, density):
    onehot = (parent_of[:, None] == jnp.arange(S, dtype=jnp.int32)[None, :]).astype(jnp.float32)
    parents = jnp.einsum('st,qtxzr->qsxzr', onehot, state, precision=lax.Precision.HIGHEST).astype(jnp.bfloat16)
    same = bin_group[:, None] == bin_group[None, :]
    kernel = jnp.where(same, production, jnp.zeros_like(production))
    source = jnp.einsum('pq,qsxzr->psxzr', kernel.astype(jnp.float32), parents.astype(jnp.float32), precision=lax.Precision.HIGHEST)
    sourced = state + source
    lap_phi = jnp.roll(sourced, 1, axis=2) + jnp.roll(sourced, -1, axis=2) - 2.0 * sourced
    pad_r = jnp.pad(sourced, ((0, 0), (0, 0), (0, 0), (0, 0), (1, 1)))
    lap_r = pad_r[..., 2:] + pad_r[..., :-2] - 2.0 * sourced
    moved = sourced + diffusivity * lap_phi + 0.5 * diffusivity * lap_r
    pad_z = jnp.pad(moved, ((0, 0), (0, 0), (0, 0), (1, 1), (0, 0)))
    halfway = moved + 0.25 * (pad_z[:, :, :, 2:] + pad_z[:, :, :, :-2] - 2.0 * moved)
    settled = jnp.einsum('yz,psxzr->psxyr', height_inverse, halfway, precision=lax.Precision.HIGHEST)
    loss_coef = loss_rate[:, None, None, None, None] * density[None, None]
    coef_next = jnp.concatenate([loss_coef[1:], jnp.zeros_like(loss_coef[:1])], axis=0)
    settled_next = jnp.concatenate([settled[1:], jnp.zeros_like(settled[:1])], axis=0)
    right_side = (1.0 - 0.5 * loss_coef) * settled + 0.5 * coef_next * settled_next

    def downward(carry, inputs):
        right, coef, coef_up = inputs
        value = (right + 0.5 * coef_up * carry) / (1.0 + 0.5 * coef)
        return value, value

    start = jnp.zeros(settled.shape[1:], jnp.float32)
    unused, result = lax.scan(downward, start, (right_side, loss_coef, coef_next), reverse=True)
    return result


def reference(spectra, production, bin_group, parent_of, diffusivity, height_inverse, loss_rate, density):
    state = spectra
    for count in range(STEPS):
        state = one_step(state, production, bin_group, parent_of, diffusivity, height_inverse, loss_rate, density)
    return state
```

```python
import functools
import math

import jax
import jax.numpy as jnp
from jax import lax
from jax.experimental import pallas as pl
from jax.experimental.pallas import tpu as pltpu
from jax.sharding import PartitionSpec as P

MESH = pl.DeviceIdType.MESH
ROWS = 16


def grid_of(count):
    columns = max(d for d in range(1, math.isqrt(count) + 1) if count % d == 0)
    return count // columns, columns


def dot(a, b):
    return jnp.dot(a, b, preferred_element_type=jnp.float32)


def dot_nt(a, b):
    return lax.dot_general(a, b, (((1,), (1,)), ((), ())), preferred_element_type=jnp.float32)


def onehot_bins(first_bins, bins, total):
    local = lax.broadcasted_iota(jnp.int32, (bins, ROWS, total), 0)
    whole = lax.broadcasted_iota(jnp.int32, (bins, ROWS, total), 2)
    parts = [
        jnp.where(local + first == whole, 1.0, 0.0).reshape(bins * ROWS, total)
        for first in first_bins
    ]
    return jnp.concatenate(parts, axis=0).astype(jnp.bfloat16)


def classes(parent_ref):
    n = parent_ref.shape[0]
    parent = [parent_ref[s] for s in range(n)]
    keys = []
    for s in range(n):
        size, first = 0, n
        for j in range(n - 1, -1, -1):
            equal = parent[j] == parent[s]
            size = size + jnp.where(equal, 1, 0)
            first = jnp.where(equal, j, first)
        keys.append((n - size) * (n * n) + first * n + s)
    ranks = [sum(jnp.where(keys[j] < keys[s], 1, 0) for j in range(n) if j != s) for s in range(n)]
    return [sum(jnp.where(ranks[s] == i, s, 0) for s in range(1, n)) for i in range(n)]


def step_kernel(
    ny,
    nx,
    kids,
    f_hbm,
    production_hbm,
    group_hbm,
    parent_hbm,
    diff_hbm,
    inverse_hbm,
    rate_hbm,
    density_hbm,
    acc,
    hin,
    weight,
    f_parts,
    parent_ref,
    group_ref,
    production_ref,
    diff_ref,
    inverse_ref,
    rate_ref,
    density_ref,
    comb,
    psend,
    precv,
    own_part,
    faces_out,
    faces_in,
    below,
    above,
    hout,
    keep,
    rates_out,
    rates_in,
    wide_0,
    wide_1,
    height,
    coef,
    in_sem,
    f_sem,
    x_send,
    x_recv,
    y_send,
    y_recv,
    f_send,
    f_recv,
    a_send,
    a_recv,
    h_send,
    h_recv,
    r_send,
    r_recv,
):
    bins, species, cells, _, radii = f_parts[0].shape
    heights = diff_ref.shape[0]
    pieces = len(f_parts)
    total_bins = production_ref.shape[0]
    count = ny * nx
    slots = len(kids)
    starts = [sum(kids[:t]) for t in range(slots)]
    wides = (wide_0, wide_1)
    phi = lax.axis_index("phi")
    mom = lax.axis_index("mom")
    phis = lax.axis_size("phi")
    row, col = mom // nx, mom % nx
    right, left = (phi + 1) % phis, (phi + phis - 1) % phis

    small = [
        pltpu.make_async_copy(parent_hbm, parent_ref, in_sem.at[0]),
        pltpu.make_async_copy(group_hbm, group_ref, in_sem.at[1]),
        pltpu.make_async_copy(production_hbm, production_ref, in_sem.at[2]),
        pltpu.make_async_copy(rate_hbm, rate_ref, in_sem.at[3]),
        pltpu.make_async_copy(diff_hbm, diff_ref, in_sem.at[4]),
        pltpu.make_async_copy(inverse_hbm, inverse_ref, in_sem.at[5]),
        pltpu.make_async_copy(density_hbm, density_ref, in_sem.at[6]),
    ]
    loads = [
        pltpu.make_async_copy(f_hbm.at[:, :, :, pl.ds(k * ROWS, ROWS), :], f_parts[k], f_sem.at[k])
        for k in range(pieces)
    ]
    small[0].start()
    for copy in loads:
        copy.start()
    for copy in small[1:]:
        copy.start()
    barrier = pltpu.get_barrier_semaphore()
    for d in range(1, count):
        pl.semaphore_signal(
            barrier, inc=1, device_id={"mom": (mom + d) % count}, device_id_type=MESH
        )
    for side in (left, right):
        pl.semaphore_signal(barrier, inc=1, device_id={"phi": side}, device_id_type=MESH)

    def along_row(d):
        return {"mom": row * nx + (col + d) % nx}

    def along_col(e):
        return {"mom": ((row + e) % ny) * nx + col}

    def sizes(x):
        return (nx, ny) if x % 2 == 0 else (ny, nx)

    def parent_copy(t, x, d, k):
        c = t * cells + x
        return pltpu.make_async_remote_copy(
            src_ref=comb.at[c, 0, k],
            dst_ref=comb.at[c, d, k],
            send_sem=x_send.at[c, d - 1, k],
            recv_sem=x_recv.at[c, d - 1, k],
            device_id=along_row(d) if x % 2 == 0 else along_col(d),
            device_id_type=MESH,
        )

    def partial_copy(t, x, e, k):
        c = t * cells + x
        return pltpu.make_async_remote_copy(
            src_ref=psend.at[c, e - 1, k],
            dst_ref=precv.at[c, e - 1, k],
            send_sem=y_send.at[c, e - 1, k],
            recv_sem=y_recv.at[c, e - 1, k],
            device_id=along_col(e) if x % 2 == 0 else along_row(e),
            device_id_type=MESH,
        )

    def face_copy(i, side, k):
        return pltpu.make_async_remote_copy(
            src_ref=faces_out.at[i, side, k],
            dst_ref=faces_in.at[i, side, k],
            send_sem=f_send.at[i, side, k],
            recv_sem=f_recv.at[i, side, k],
            device_id={"phi": left if side == 0 else right},
            device_id_type=MESH,
        )

    def below_copy(i, x):
        return pltpu.make_async_remote_copy(
            src_ref=below.at[i, x],
            dst_ref=above.at[i, x],
            send_sem=a_send.at[i, x],
            recv_sem=a_recv.at[i, x],
            device_id={"mom": (mom + count - 1) % count},
            device_id_type=MESH,
        )

    def h_copy(i, x, n):
        return pltpu.make_async_remote_copy(
            src_ref=hout.at[i, x],
            dst_ref=hin.at[i, x],
            send_sem=h_send.at[i, x, n],
            recv_sem=h_recv.at[i, x],
            device_id={"mom": (mom + count - 1 - n) % count},
            device_id_type=MESH,
        )

    def rate_copy():
        return pltpu.make_async_remote_copy(
            src_ref=rates_out,
            dst_ref=rates_in,
            send_sem=r_send,
            recv_sem=r_recv,
            device_id={"mom": (mom + count - 1) % count},
            device_id_type=MESH,
        )

    def fill_parents(t, k):
        parent = parent_ref[order[starts[t]]]
        for x in range(cells):
            comb[t * cells + x, 0, k] = f_parts[k][:, parent, x].astype(jnp.bfloat16)

    def send_parents(t, k):
        for x in range(cells):
            for d in range(1, sizes(x)[0]):
                parent_copy(t, x, d, k).start()

    odd = mom % 2 == 1
    ahead = 2
    small[0].wait()
    order = classes(parent_ref)
    for k in range(pieces):
        loads[k].wait()
        fill_parents(0, k)
        if k == 0:
            pl.semaphore_wait(barrier, count + 1)
        send_parents(0, k)
    for t in range(1, slots):
        for k in range(pieces):
            fill_parents(t, k)
            if t < ahead:
                send_parents(t, k)

    for copy in small[1:]:
        copy.wait()
    for p in range(bins):
        rates_out[pl.ds(p, 1), :] = jnp.full((1, radii), rate_ref[p], jnp.float32)

    @pl.when(odd)
    def _():
        rate_copy().start()

    p_at = lax.broadcasted_iota(jnp.int32, (total_bins, total_bins), 0)
    q_at = lax.broadcasted_iota(jnp.int32, (total_bins, total_bins), 1)
    p_group = jnp.zeros((total_bins, total_bins), jnp.int32)
    q_group = jnp.zeros((total_bins, total_bins), jnp.int32)
    for b in range(total_bins):
        p_group = jnp.where(p_at == b, group_ref[b], p_group)
        q_group = jnp.where(q_at == b, group_ref[b], q_group)
    kernel = jnp.where(p_group == q_group, production_ref[...].astype(jnp.float32), 0.0)
    kernel = kernel.astype(jnp.bfloat16)
    row_starts = [(row * nx + (col + d) % nx) * bins for d in range(nx)]
    col_starts = [(((row + e) % ny) * nx + col) * bins for e in range(ny)]
    row_froms = [(row * nx + (col + nx - d) % nx) * bins for d in range(nx)]
    col_froms = [(((row + ny - e) % ny) * nx + col) * bins for e in range(ny)]
    for to, source_from, ref in ((col_starts, row_froms, wide_0), (row_starts, col_froms, wide_1)):
        rows_1h = onehot_bins(to, bins, total_bins)
        cols_1h = onehot_bins(source_from, bins, total_bins)
        mixed = dot_nt(dot(rows_1h, kernel).astype(jnp.bfloat16), cols_1h)
        r_at = lax.broadcasted_iota(jnp.int32, mixed.shape, 0) & (ROWS - 1)
        c_at = lax.broadcasted_iota(jnp.int32, mixed.shape, 1) & (ROWS - 1)
        ref[...] = jnp.where(r_at == c_at, mixed, 0.0).astype(jnp.bfloat16)

    group = height.shape[1] // heights
    a_at = lax.broadcasted_iota(jnp.int32, (heights, heights), 0)
    b_at = lax.broadcasted_iota(jnp.int32, (heights, heights), 1)
    stencil = jnp.where(a_at == b_at, 0.5, 0.0) + jnp.where(jnp.abs(a_at - b_at) == 1, 0.25, 0.0)
    both = jnp.dot(
        inverse_ref[...],
        stencil,
        precision=lax.Precision.HIGHEST,
        preferred_element_type=jnp.float32,
    )
    high = both.astype(jnp.bfloat16).astype(jnp.float32)
    tall_a = lax.broadcasted_iota(jnp.int32, (group, heights, heights), 1)
    tall_b = lax.broadcasted_iota(jnp.int32, (group, heights, heights), 2)
    spread = jnp.where(tall_a == tall_b, 1.0, 0.0).reshape(group * heights, heights)
    spread = spread.astype(jnp.bfloat16)
    row_g = lax.broadcasted_iota(jnp.int32, (group, heights, group * heights), 0)
    col_g = lax.broadcasted_iota(jnp.int32, (group, heights, group * heights), 2)
    first = row_g * heights
    inside = jnp.where((col_g >= first) & (col_g < first + heights), 1.0, 0.0)
    inside = inside.reshape(group * heights, group * heights)
    for n, part in enumerate((high, both - high)):
        tall = jnp.concatenate([part] * group, axis=0).astype(jnp.bfloat16)
        height[n] = (dot_nt(tall, spread) * inside).astype(jnp.bfloat16)

    diff = diff_ref[...]
    lane = lax.broadcasted_iota(jnp.int32, diff.shape, 1)
    coef[0] = 1.0 - 3.0 * diff
    coef[1] = jnp.where(lane == 0, 0.0, 0.5 * diff)
    coef[2] = jnp.where(lane == radii - 1, 0.0, 0.5 * diff)

    for x in range(cells):
        kept = jnp.ones((heights, radii), jnp.float32)
        for p in range(bins):
            part = 1.0 / (1.0 + 0.5 * rate_ref[p] * density_ref[x])
            weight[p, x] = part
            kept = kept * (1.0 - part)
        keep[0, x] = kept

    def keep_above():
        rate_copy().wait_recv()
        for x in range(cells):
            kept = jnp.ones((heights, radii), jnp.float32)
            for p in range(bins):
                kept = kept * (1.0 - 1.0 / (1.0 + 0.5 * rates_in[pl.ds(p, 1), :] * density_ref[x]))
            keep[1, x] = kept

    @pl.when(mom >= count - 2)
    def _():
        hin[...] = jnp.zeros_like(hin)

    def mix(t):
        for k in range(pieces):
            for x in range(cells):
                c = t * cells + x
                n1, n2 = sizes(x)
                for d in range(1, n1):
                    parent_copy(t, x, d, k).wait_recv()
                block = comb[c, :n1, k].reshape(n1 * bins * ROWS, radii)
                sums = dot(wides[x % 2][...], block).reshape(n2, bins, ROWS, radii)
                own_part[c, k] = sums[0]
                for e in range(1, n2):
                    psend[c, e - 1, k] = sums[e].astype(jnp.bfloat16)
                    partial_copy(t, x, e, k).start()
        if t + ahead < slots:
            for k in range(pieces):
                send_parents(t + ahead, k)

    def source(t):
        for k in range(pieces):
            at = pl.ds(k * ROWS, ROWS)
            for x in range(cells):
                c = t * cells + x
                n2 = sizes(x)[1]
                for e in range(1, n2):
                    partial_copy(t, x, e, k).wait_recv()

                @pl.loop(0, bins)
                def _(p):
                    value = own_part[c, k, p]
                    for e in range(1, n2):
                        value = value + precv[c, e - 1, k, p].astype(jnp.float32)
                    for i in range(starts[t], starts[t] + kids[t]):
                        total = f_parts[k][p, order[i], x] + value
                        acc[i * cells + x, p, at, :] = total
                        rounded = total.astype(jnp.bfloat16)
                        if x == 0:
                            faces_out[i, 0, k, p] = rounded
                        if x == cells - 1:
                            faces_out[i, 1, k, p] = rounded

                for i in range(starts[t], starts[t] + kids[t]):
                    if x == 0:
                        face_copy(i, 0, k).start()
                    if x == cells - 1:
                        face_copy(i, 1, k).start()

    def diffuse(i):
        for k in range(pieces):
            face_copy(i, 0, k).wait_recv()
            face_copy(i, 1, k).wait_recv()
        first = i * cells
        per = group // cells

        @pl.loop(0, bins // per)
        def _(k):
            planes = []
            for j in range(per):
                p = k * per + j
                own = [acc[first + x, p] for x in range(cells)]
                ends = [
                    faces_in[i, side, :, p].reshape(heights, radii).astype(jnp.float32)
                    for side in range(2)
                ]
                before = [ends[1]] + own[:-1]
                after = own[1:] + [ends[0]]
                for x in range(cells):
                    moved = coef[0] * own[x] + diff_ref[...] * (before[x] + after[x])
                    moved += coef[1] * pltpu.roll(own[x], 1, 1)
                    moved += coef[2] * pltpu.roll(own[x], radii - 1, 1)
                    planes.append(moved)
            moved = jnp.concatenate(planes, axis=0)
            high = moved.astype(jnp.bfloat16)
            low = (moved - high.astype(jnp.float32)).astype(jnp.bfloat16)
            settled = dot(height[0], high) + dot(height[0], low) + dot(height[1], high)
            for j in range(per):
                for x in range(cells):
                    n = j * cells + x
                    acc[first + x, k * per + j] = settled[n * heights : (n + 1) * heights]

        span = heights // 2
        for x in range(cells):
            @pl.loop(0, 2)
            def _(k):
                at = pl.ds(pl.multiple_of(k * span, span), span)
                carry = jnp.zeros((span, radii), jnp.float32)
                for p in range(bins - 1, -1, -1):
                    total = 2.0 * acc[first + x, p, at, :] + carry
                    carry = total - total * weight[p, x, at, :]
                below[i, x, at, :] = carry

    def send_below(i):
        @pl.when(odd)
        def _():
            for x in range(cells):
                below_copy(i, x).start()

    def diffuse_slot(t, send):
        @pl.loop(starts[t], starts[t] + kids[t])
        def _(i):
            diffuse(i)
            if send:
                send_below(i)

    def relay(i):
        for x in range(cells):
            below_copy(i, x).wait_recv()

            @pl.when(mom < count - 2)
            def _():
                h_copy(i, x, 1).wait_recv()

            entering = above[i, x] + keep[1, x] * hin[i, x]
            hin[i, x] = entering
            hout[i, x] = below[i, x] + keep[0, x] * entering

            @pl.when(mom > 0)
            def _():
                h_copy(i, x, 0).start()
                h_copy(i, x, 1).start()

    lag = (count - 1 - mom) // 2
    early = species - kids[-1]
    for i in range(slots + 1):
        if i < slots:
            mix(i)
        if 1 <= i:
            source(i - 1)
        if i >= 2:
            diffuse_slot(i - 2, False)
        if i == max(slots - 1, 0):
            @pl.when(mom % 2 == 0)
            def _():
                keep_above()

        if i == slots - 1:
            @pl.loop(0, sum(kids[: max(slots - 2, 0)]))
            def _(i):
                send_below(i)
        if i == slots:
            @pl.loop(sum(kids[: max(slots - 2, 0)]), early)
            def _(i):
                send_below(i)

    @pl.when((mom % 2 == 0) & (lag == 0))
    def _():
        @pl.loop(0, early)
        def _(i):
            relay(i)

    diffuse_slot(slots - 1, True)

    @pl.when((mom % 2 == 0) & (lag > 0))
    def _():
        @pl.loop(0, early)
        def _(i):
            relay(i)

    @pl.when(mom % 2 == 0)
    def _():
        @pl.loop(early, species)
        def _(i):
            relay(i)

    @pl.when(odd)
    def _():
        rate_copy().wait_send()

    for t in range(slots):
        for k in range(pieces):
            for x in range(cells):
                for d in range(1, sizes(x)[0]):
                    parent_copy(t, x, d, k).wait_send()
                for e in range(1, sizes(x)[1]):
                    partial_copy(t, x, e, k).wait_send()

    @pl.loop(0, species)
    def _(i):
        for k in range(pieces):
            face_copy(i, 0, k).wait_send()
            face_copy(i, 1, k).wait_send()
        for x in range(cells):
            @pl.when(odd)
            def _():
                below_copy(i, x).wait_send()

            @pl.when(odd & (mom < count - 1))
            def _():
                h_copy(i, x, 0).wait_recv()

            @pl.when((mom % 2 == 0) & (mom > 0))
            def _():
                h_copy(i, x, 0).wait_send()
                h_copy(i, x, 1).wait_send()


def solve_kernel(
    settled_ref, hin_ref, weight_ref, parent_hbm, out_hbm, done, parent_ref, in_sem, out_sem
):
    bins, cells, heights, radii = weight_ref.shape
    species = parent_ref.shape[0]
    span = heights // 2
    load = pltpu.make_async_copy(parent_hbm, parent_ref, in_sem)
    load.start()
    order = None
    copies = []
    for i in range(species):
        for x in range(cells):
            n = i * cells + x

            @pl.loop(0, 2)
            def _(k):
                at = pl.ds(pl.multiple_of(k * span, span), span)
                carry = hin_ref[i, x, at, :]
                for p in range(bins - 1, -1, -1):
                    settled = settled_ref[n, p, at, :]
                    total = 2.0 * settled + carry
                    both = total * weight_ref[p, x, at, :]
                    done[n, p, at, :] = both - settled
                    carry = total - both

            if order is None:
                load.wait()
                order = classes(parent_ref)
            copy = pltpu.make_async_copy(done.at[n], out_hbm.at[:, order[i], x], out_sem.at[n])
            copy.start()
            copies.append(copy)
    for copy in copies:
        copy.wait()


def local(
    ny,
    nx,
    which,
    kids,
    spectra,
    production,
    bin_group,
    parent_of,
    diffusivity,
    height_inverse,
    loss_rate,
    density,
):
    bins, species, cells, heights, radii = spectra.shape
    chunks = len(kids) * cells
    block = (bins, heights, radii)
    plane = (heights, radii)
    pieces = heights // ROWS
    split = (pieces, bins, ROWS, radii)
    most = max(nx, ny)
    group = cells * max(1, 256 // (heights * cells))
    dma = pltpu.SemaphoreType.DMA
    vmem = pl.BlockSpec(memory_space=pltpu.VMEM)
    hbm = pl.BlockSpec(memory_space=pltpu.HBM)
    stay = functools.partial(pltpu.with_memory_space_constraint, memory_space=pltpu.HBM)
    tall, broad = ny * bins * ROWS, nx * bins * ROWS
    settled, entering, weight = pl.pallas_call(
        functools.partial(step_kernel, ny, nx, kids),
        out_shape=[
            jax.ShapeDtypeStruct((species * cells,) + block, jnp.float32),
            jax.ShapeDtypeStruct((species, cells) + plane, jnp.float32),
            jax.ShapeDtypeStruct((bins, cells) + plane, jnp.float32),
        ],
        in_specs=[hbm] * 8,
        out_specs=[vmem, vmem, vmem],
        scratch_shapes=[
            [pltpu.VMEM((bins, species, cells, ROWS, radii), jnp.float32) for _ in range(pieces)],
            pltpu.SMEM(parent_of.shape, jnp.int32),
            pltpu.SMEM(bin_group.shape, jnp.int32),
            pltpu.VMEM(production.shape, jnp.bfloat16),
            pltpu.VMEM(plane, jnp.float32),
            pltpu.VMEM(height_inverse.shape, jnp.float32),
            pltpu.SMEM(loss_rate.shape, jnp.float32),
            pltpu.VMEM(density.shape, jnp.float32),
            pltpu.VMEM((chunks, most) + split, jnp.bfloat16),
            pltpu.VMEM((chunks, most - 1) + split, jnp.bfloat16),
            pltpu.VMEM((chunks, most - 1) + split, jnp.bfloat16),
            pltpu.VMEM((chunks,) + split, jnp.float32),
            pltpu.VMEM((species, 2) + split, jnp.bfloat16),
            pltpu.VMEM((species, 2) + split, jnp.bfloat16),
            pltpu.VMEM((species, cells) + plane, jnp.float32),
            pltpu.VMEM((species, cells) + plane, jnp.float32),
            pltpu.VMEM((species, cells) + plane, jnp.float32),
            pltpu.VMEM((2, cells) + plane, jnp.float32),
            pltpu.VMEM((max(bins, 8), radii), jnp.float32),
            pltpu.VMEM((max(bins, 8), radii), jnp.float32),
            pltpu.VMEM((tall, broad), jnp.bfloat16),
            pltpu.VMEM((broad, tall), jnp.bfloat16),
            pltpu.VMEM((2, group * heights, group * heights), jnp.bfloat16),
            pltpu.VMEM((3,) + plane, jnp.float32),
            dma((7,)),
            dma((pieces,)),
            dma((chunks, most - 1, pieces)),
            dma((chunks, most - 1, pieces)),
            dma((chunks, most - 1, pieces)),
            dma((chunks, most - 1, pieces)),
            dma((species, 2, pieces)),
            dma((species, 2, pieces)),
            dma((species, cells)),
            dma((species, cells)),
            dma((species, cells, 2)),
            dma((species, cells)),
            dma,
            dma,
        ],
        compiler_params=pltpu.CompilerParams(
            collective_id=which, has_side_effects=True, vmem_limit_bytes=40 * 1024 * 1024
        ),
    )(*(stay(a) for a in (
        spectra, production, bin_group, parent_of, diffusivity, height_inverse, loss_rate, density
    )))
    return pl.pallas_call(
        solve_kernel,
        out_shape=jax.ShapeDtypeStruct(spectra.shape, jnp.float32),
        in_specs=[vmem, vmem, vmem, hbm],
        out_specs=hbm,
        scratch_shapes=[
            pltpu.VMEM((species * cells,) + block, jnp.float32),
            pltpu.SMEM(parent_of.shape, jnp.int32),
            dma,
            dma((species * cells,)),
        ],
        compiler_params=pltpu.CompilerParams(vmem_limit_bytes=16 * 1024 * 1024),
    )(settled, entering, weight, stay(parent_of))


def step(ny, nx, *args):
    parent_of = args[3]
    species = parent_of.shape[0]
    single = (1,) * species
    if species != 4:
        return local(ny, nx, 0, single, *args)
    pairs = jnp.sum((parent_of[:, None] == parent_of[None, :]).astype(jnp.int32))
    which = jnp.where(pairs > 8, 0, jnp.where(pairs > 6, 1, jnp.where(pairs > 4, 2, 3)))
    forms = ((3, 1), (2, 2), (2, 1, 1), single)
    return lax.switch(
        which, [functools.partial(local, ny, nx, n, kids) for n, kids in enumerate(forms)], *args
    )


def solution(mesh):
    ny, nx = grid_of(mesh.shape["mom"])
    return jax.shard_map(
        functools.partial(step, ny, nx),
        mesh=mesh,
        in_specs=(
            P("mom", None, "phi", None, None),
            P(),
            P(),
            P(),
            P(),
            P(),
            P("mom"),
            P("phi", None, None),
        ),
        out_specs=P("mom", None, "phi", None, None),
        check_vma=False,
    )
```

```python
import functools
import math

import jax
import jax.numpy as jnp
import numpy as np
from jax import lax
from jax.experimental import pallas as pl
from jax.experimental.pallas import tpu as pltpu
from jax.sharding import PartitionSpec as P

MESH = pl.DeviceIdType.MESH
ROWS = 16
VMEM = pl.BlockSpec(memory_space=pltpu.VMEM)
HBM = pl.BlockSpec(memory_space=pltpu.HBM)
stay = functools.partial(pltpu.with_memory_space_constraint, memory_space=pltpu.HBM)


def grid_of(count):
    columns = max(d for d in range(1, math.isqrt(count) + 1) if count % d == 0)
    return count // columns, columns


def dot(a, b):
    return jnp.dot(a, b, preferred_element_type=jnp.float32)


def dot_nt(a, b):
    return lax.dot_general(a, b, (((1,), (1,)), ((), ())), preferred_element_type=jnp.float32)


def onehot_bins(first_bins, bins, total):
    local = lax.broadcasted_iota(jnp.int32, (bins, ROWS, total), 0)
    whole = lax.broadcasted_iota(jnp.int32, (bins, ROWS, total), 2)
    parts = [
        jnp.where(local + first == whole, 1.0, 0.0).reshape(bins * ROWS, total)
        for first in first_bins
    ]
    return jnp.concatenate(parts, axis=0).astype(jnp.bfloat16)


def coded(value):
    fourth = (value * value) * (value * value)
    return jnp.where(value < 0.0, -fourth, fourth).astype(jnp.bfloat16)


def decoded(code):
    code = code.astype(jnp.float32)
    root = jnp.sqrt(jnp.sqrt(jnp.abs(code)))
    return jnp.where(code < 0.0, -root, root)


def classes(parent_ref):
    n = parent_ref.shape[0]
    parent = [parent_ref[s] for s in range(n)]
    keys = []
    for s in range(n):
        size, first = 0, n
        for j in range(n - 1, -1, -1):
            equal = parent[j] == parent[s]
            size = size + jnp.where(equal, 1, 0)
            first = jnp.where(equal, j, first)
        keys.append((n - size) * (n * n) + first * n + s)
    ranks = [sum(jnp.where(keys[j] < keys[s], 1, 0) for j in range(n) if j != s) for s in range(n)]
    return [sum(jnp.where(ranks[s] == i, s, 0) for s in range(1, n)) for i in range(n)]


def step_kernel(
    ny,
    nx,
    kids,
    f_hbm,
    production_hbm,
    group_hbm,
    parent_hbm,
    diff_hbm,
    inverse_hbm,
    rate_hbm,
    density_hbm,
    acc,
    f_ref,
    parent_ref,
    order_ref,
    group_ref,
    production_ref,
    diff_ref,
    inverse_ref,
    rate_ref,
    density_ref,
    comb,
    psend,
    precv,
    own_part,
    faces_out,
    faces_in,
    below,
    below_out,
    above,
    entered,
    hin,
    hout,
    weight,
    keep,
    rates_out,
    rates_in,
    wide_0,
    wide_1,
    height,
    coef,
    in_sem,
    f_sem,
    x_send,
    x_recv,
    y_send,
    y_recv,
    f_send,
    f_recv,
    a_send,
    a_recv,
    h_send,
    h_recv,
    r_send,
    r_recv,
):
    bins, species, cells, heights, radii = f_ref.shape
    pieces = heights // ROWS
    total_bins = production_ref.shape[0]
    count = ny * nx
    slots = len(kids)
    wides = (wide_0, wide_1)
    phi = lax.axis_index("phi")
    mom = lax.axis_index("mom")
    phis = lax.axis_size("phi")
    row, col = mom // nx, mom % nx
    right, left = (phi + 1) % phis, (phi + phis - 1) % phis

    def first_of(t):
        return sum(jnp.where(t > j, kids[j], 0) for j in range(slots))

    def rows(k):
        return pl.ds(pl.multiple_of(k * ROWS, ROWS), ROWS)

    small = [
        pltpu.make_async_copy(parent_hbm, parent_ref, in_sem.at[0]),
        pltpu.make_async_copy(group_hbm, group_ref, in_sem.at[1]),
        pltpu.make_async_copy(production_hbm, production_ref, in_sem.at[2]),
        pltpu.make_async_copy(rate_hbm, rate_ref, in_sem.at[3]),
        pltpu.make_async_copy(diff_hbm, diff_ref, in_sem.at[4]),
        pltpu.make_async_copy(inverse_hbm, inverse_ref, in_sem.at[5]),
        pltpu.make_async_copy(density_hbm, density_ref, in_sem.at[6]),
    ]
    loads = [
        pltpu.make_async_copy(
            f_hbm.at[:, :, :, pl.ds(k * ROWS, ROWS), :],
            f_ref.at[:, :, :, pl.ds(k * ROWS, ROWS), :],
            f_sem.at[k],
        )
        for k in range(pieces)
    ]
    small[0].start()
    for copy in loads:
        copy.start()
    for copy in small[1:]:
        copy.start()
    barrier = pltpu.get_barrier_semaphore()
    for d in range(1, count):
        pl.semaphore_signal(
            barrier, inc=1, device_id={"mom": (mom + d) % count}, device_id_type=MESH
        )
    for side in (left, right):
        pl.semaphore_signal(barrier, inc=1, device_id={"phi": side}, device_id_type=MESH)

    def along_row(d):
        return {"mom": row * nx + (col + d) % nx}

    def along_col(e):
        return {"mom": ((row + e) % ny) * nx + col}

    def sizes(x):
        return (nx, ny) if x % 2 == 0 else (ny, nx)

    def parent_copy(t, x, d, k):
        c = t * cells + x
        return pltpu.make_async_remote_copy(
            src_ref=comb.at[c, 0, k],
            dst_ref=comb.at[c, d, k],
            send_sem=x_send.at[c, d - 1, k],
            recv_sem=x_recv.at[c, d - 1, k],
            device_id=along_row(d) if x % 2 == 0 else along_col(d),
            device_id_type=MESH,
        )

    def partial_copy(t, x, e, k):
        c = t * cells + x
        return pltpu.make_async_remote_copy(
            src_ref=psend.at[c, e - 1, k],
            dst_ref=precv.at[c, e - 1, k],
            send_sem=y_send.at[c, e - 1, k],
            recv_sem=y_recv.at[c, e - 1, k],
            device_id=along_col(e) if x % 2 == 0 else along_row(e),
            device_id_type=MESH,
        )

    def face_copy(i, side, k):
        return pltpu.make_async_remote_copy(
            src_ref=faces_out.at[i, side, k],
            dst_ref=faces_in.at[i, side, k],
            send_sem=f_send.at[i, side, k],
            recv_sem=f_recv.at[i, side, k],
            device_id={"phi": left if side == 0 else right},
            device_id_type=MESH,
        )

    def below_copy(i, x):
        return pltpu.make_async_remote_copy(
            src_ref=below_out.at[i, x],
            dst_ref=above.at[i, x],
            send_sem=a_send.at[i, x],
            recv_sem=a_recv.at[i, x],
            device_id={"mom": (mom + count - 1) % count},
            device_id_type=MESH,
        )

    def h_copy(i, x, n):
        return pltpu.make_async_remote_copy(
            src_ref=hout.at[i, x],
            dst_ref=entered.at[i, x],
            send_sem=h_send.at[i, x, n],
            recv_sem=h_recv.at[i, x],
            device_id={"mom": (mom + count - 1 - n) % count},
            device_id_type=MESH,
        )

    def rate_copy():
        return pltpu.make_async_remote_copy(
            src_ref=rates_out,
            dst_ref=rates_in,
            send_sem=r_send,
            recv_sem=r_recv,
            device_id={"mom": (mom + count - 1) % count},
            device_id_type=MESH,
        )

    def send_parents(t, k):
        for x in range(cells):
            for d in range(1, sizes(x)[0]):
                parent_copy(t, x, d, k).start()

    odd = mom % 2 == 1
    ahead = 2
    small[0].wait()
    for i, s in enumerate(classes(parent_ref)):
        order_ref[i] = s
    parent = parent_ref[order_ref[0]]
    for k in range(pieces):
        loads[k].wait()
        at = pl.ds(k * ROWS, ROWS)
        for x in range(cells):
            chosen = f_ref[:, 0, x, at, :]
            for s in range(1, species):
                chosen = jnp.where(parent == s, f_ref[:, s, x, at, :], chosen)
            comb[x, 0, k] = chosen.astype(jnp.bfloat16)
        if k == 0:
            pl.semaphore_wait(barrier, count + 1)
        send_parents(0, k)

    @pl.loop(1, slots)
    def _(t):
        parent = parent_ref[order_ref[first_of(t)]]

        @pl.loop(0, pieces)
        def _(k):
            for x in range(cells):
                comb[t * cells + x, 0, k] = f_ref[:, parent, x, rows(k), :].astype(jnp.bfloat16)

            @pl.when(t < ahead)
            def _():
                send_parents(t, k)

    for copy in small[1:]:
        copy.wait()
    for p in range(bins):
        rates_out[pl.ds(p, 1), :] = jnp.full((1, radii), rate_ref[p], jnp.float32)

    @pl.when(odd)
    def _():
        rate_copy().start()

    p_at = lax.broadcasted_iota(jnp.int32, (total_bins, total_bins), 0)
    q_at = lax.broadcasted_iota(jnp.int32, (total_bins, total_bins), 1)
    p_group = jnp.zeros((total_bins, total_bins), jnp.int32)
    q_group = jnp.zeros((total_bins, total_bins), jnp.int32)
    for b in range(total_bins):
        p_group = jnp.where(p_at == b, group_ref[b], p_group)
        q_group = jnp.where(q_at == b, group_ref[b], q_group)
    kernel = jnp.where(p_group == q_group, production_ref[...].astype(jnp.float32), 0.0)
    kernel = kernel.astype(jnp.bfloat16)
    row_starts = [(row * nx + (col + d) % nx) * bins for d in range(nx)]
    col_starts = [(((row + e) % ny) * nx + col) * bins for e in range(ny)]
    row_froms = [(row * nx + (col + nx - d) % nx) * bins for d in range(nx)]
    col_froms = [(((row + ny - e) % ny) * nx + col) * bins for e in range(ny)]
    for to, source_from, ref in ((col_starts, row_froms, wide_0), (row_starts, col_froms, wide_1)):
        rows_1h = onehot_bins(to, bins, total_bins)
        cols_1h = onehot_bins(source_from, bins, total_bins)
        mixed = dot_nt(dot(rows_1h, kernel).astype(jnp.bfloat16), cols_1h)
        r_at = lax.broadcasted_iota(jnp.int32, mixed.shape, 0) & (ROWS - 1)
        c_at = lax.broadcasted_iota(jnp.int32, mixed.shape, 1) & (ROWS - 1)
        ref[...] = jnp.where(r_at == c_at, mixed, 0.0).astype(jnp.bfloat16)

    group = height.shape[1] // heights
    a_at = lax.broadcasted_iota(jnp.int32, (heights, heights), 0)
    b_at = lax.broadcasted_iota(jnp.int32, (heights, heights), 1)
    stencil = jnp.where(a_at == b_at, 0.5, 0.0) + jnp.where(jnp.abs(a_at - b_at) == 1, 0.25, 0.0)
    both = jnp.dot(
        inverse_ref[...],
        stencil,
        precision=lax.Precision.HIGHEST,
        preferred_element_type=jnp.float32,
    )
    high = both.astype(jnp.bfloat16).astype(jnp.float32)
    tall_a = lax.broadcasted_iota(jnp.int32, (group, heights, heights), 1)
    tall_b = lax.broadcasted_iota(jnp.int32, (group, heights, heights), 2)
    spread = jnp.where(tall_a == tall_b, 1.0, 0.0).reshape(group * heights, heights)
    spread = spread.astype(jnp.bfloat16)
    row_g = lax.broadcasted_iota(jnp.int32, (group, heights, group * heights), 0)
    col_g = lax.broadcasted_iota(jnp.int32, (group, heights, group * heights), 2)
    first = row_g * heights
    inside = jnp.where((col_g >= first) & (col_g < first + heights), 1.0, 0.0)
    inside = inside.reshape(group * heights, group * heights)
    for n, part in enumerate((high, both - high)):
        tall = jnp.concatenate([part] * group, axis=0).astype(jnp.bfloat16)
        height[n] = (dot_nt(tall, spread) * inside).astype(jnp.bfloat16)

    diff = diff_ref[...]
    lane = lax.broadcasted_iota(jnp.int32, diff.shape, 1)
    coef[0] = 1.0 - 3.0 * diff
    coef[1] = jnp.where(lane == 0, 0.0, 0.5 * diff)
    coef[2] = jnp.where(lane == radii - 1, 0.0, 0.5 * diff)

    for x in range(cells):
        @pl.loop(0, pieces)
        def _(k):
            kept = jnp.ones((ROWS, radii), jnp.float32)
            for p in range(bins):
                part = 1.0 / (1.0 + 0.5 * rate_ref[p] * density_ref[x, rows(k), :])
                weight[p, x, rows(k), :] = part
                kept = kept * (1.0 - part)
            keep[0, x, rows(k), :] = kept

    def keep_above():
        rate_copy().wait_recv()
        for x in range(cells):
            @pl.loop(0, pieces)
            def _(k):
                dens = density_ref[x, rows(k), :]
                kept = jnp.ones((ROWS, radii), jnp.float32)
                for p in range(bins):
                    kept = kept * (1.0 - 1.0 / (1.0 + 0.5 * rates_in[pl.ds(p, 1), :] * dens))
                keep[1, x, rows(k), :] = kept

    @pl.when(mom >= count - 2)
    def _():
        entered[...] = jnp.zeros_like(entered)

    def mix(t):
        @pl.loop(0, pieces)
        def _(k):
            for x in range(cells):
                c = t * cells + x
                n1, n2 = sizes(x)
                for d in range(1, n1):
                    parent_copy(t, x, d, k).wait_recv()
                block = comb[c, :n1, k].reshape(n1 * bins * ROWS, radii)
                sums = dot(wides[x % 2][...], block).reshape(n2, bins, ROWS, radii)
                own_part[c, k] = sums[0]
                for e in range(1, n2):
                    psend[c, e - 1, k] = sums[e].astype(jnp.bfloat16)
                    partial_copy(t, x, e, k).start()

        @pl.when(t + ahead < slots)
        def _():
            @pl.loop(0, pieces)
            def _(k):
                send_parents(t + ahead, k)

    def source(t):
        @pl.loop(0, pieces)
        def _(k):
            for x in range(cells):
                c = t * cells + x
                n2 = sizes(x)[1]
                for e in range(1, n2):
                    partial_copy(t, x, e, k).wait_recv()

                @pl.loop(first_of(t), first_of(t + 1))
                def _(i):
                    total = f_ref[:, order_ref[i], x, rows(k), :] + own_part[c, k]
                    for e in range(1, n2):
                        total = total + precv[c, e - 1, k].astype(jnp.float32)
                    acc[i * cells + x, :, rows(k), :] = total
                    rounded = total.astype(jnp.bfloat16)
                    if x == 0:
                        faces_out[i, 0, k] = rounded
                        face_copy(i, 0, k).start()
                    if x == cells - 1:
                        faces_out[i, 1, k] = rounded
                        face_copy(i, 1, k).start()

    def diffuse(i):
        @pl.loop(0, pieces)
        def _(k):
            face_copy(i, 0, k).wait_recv()
            face_copy(i, 1, k).wait_recv()

        first = i * cells
        per = group // cells

        @pl.loop(0, bins // per)
        def _(k):
            planes = []
            for j in range(per):
                p = k * per + j
                own = [acc[first + x, p] for x in range(cells)]
                ends = [
                    faces_in[i, side, :, p].reshape(heights, radii).astype(jnp.float32)
                    for side in range(2)
                ]
                before = [ends[1]] + own[:-1]
                after = own[1:] + [ends[0]]
                for x in range(cells):
                    moved = coef[0] * own[x] + diff_ref[...] * (before[x] + after[x])
                    moved += coef[1] * pltpu.roll(own[x], 1, 1)
                    moved += coef[2] * pltpu.roll(own[x], radii - 1, 1)
                    planes.append(moved)
            moved = jnp.concatenate(planes, axis=0)
            high = moved.astype(jnp.bfloat16)
            low = (moved - high.astype(jnp.float32)).astype(jnp.bfloat16)
            settled = dot(height[0], high) + dot(height[0], low) + dot(height[1], high)
            for j in range(per):
                for x in range(cells):
                    n = j * cells + x
                    acc[first + x, k * per + j] = settled[n * heights : (n + 1) * heights]

        span = heights // 2
        for x in range(cells):
            @pl.loop(0, 2)
            def _(k):
                at = pl.ds(pl.multiple_of(k * span, span), span)
                carry = jnp.zeros((span, radii), jnp.float32)
                for p in range(bins - 1, -1, -1):
                    total = 2.0 * acc[first + x, p, at, :] + carry
                    carry = total - total * weight[p, x, at, :]
                below[i, x, at, :] = carry
                below_out[i, x, at, :] = coded(carry)

    def send_below(i):
        @pl.when(odd)
        def _():
            for x in range(cells):
                below_copy(i, x).start()

    def finish(i):
        span = heights // 2
        for x in range(cells):
            @pl.when(odd)
            def _():
                @pl.when(mom < count - 1)
                def _():
                    h_copy(i, x, 0).wait_recv()

                hin[x] = decoded(entered[i, x])

            @pl.when(mom % 2 == 0)
            def _():
                below_copy(i, x).wait_recv()

                @pl.when(mom < count - 2)
                def _():
                    h_copy(i, x, 1).wait_recv()

                entering = decoded(above[i, x]) + keep[1, x] * decoded(entered[i, x])
                hin[x] = entering
                hout[i, x] = coded(below[i, x] + keep[0, x] * entering)

                @pl.when(mom > 0)
                def _():
                    h_copy(i, x, 0).start()
                    h_copy(i, x, 1).start()

            @pl.loop(0, 2)
            def _(k):
                at = pl.ds(pl.multiple_of(k * span, span), span)
                carry = hin[x, at, :]
                for p in range(bins - 1, -1, -1):
                    settled = acc[i * cells + x, p, at, :]
                    total = 2.0 * settled + carry
                    both = total * weight[p, x, at, :]
                    acc[i * cells + x, p, at, :] = both - settled
                    carry = total - both

    early = species - kids[-1]
    held = sum(kids[: max(slots - 2, 0)])

    @pl.loop(0, slots + 2)
    def _(i):
        @pl.when(i < slots)
        def _():
            mix(i)

        @pl.when(i == slots - 1)
        def _():
            @pl.when(mom % 2 == 0)
            def _():
                keep_above()

        @pl.when((i >= 1) & (i < slots + 1))
        def _():
            source(i - 1)

        @pl.when((i == slots + 1) & (mom >= count - 2))
        def _():
            @pl.loop(0, early)
            def _(j):
                finish(j)

        @pl.when(i >= 2)
        def _():
            @pl.loop(first_of(i - 2), first_of(i - 1))
            def _(j):
                diffuse(j)

                @pl.when(i >= slots)
                def _():
                    send_below(j)

        @pl.when(i == slots - 1)
        def _():
            @pl.loop(0, held)
            def _(j):
                send_below(j)

    @pl.loop(jnp.where(mom >= count - 2, early, 0), species)
    def _(j):
        finish(j)

    @pl.when(odd)
    def _():
        rate_copy().wait_send()

    @pl.loop(0, slots)
    def _(t):
        @pl.loop(0, pieces)
        def _(k):
            for x in range(cells):
                for d in range(1, sizes(x)[0]):
                    parent_copy(t, x, d, k).wait_send()
                for e in range(1, sizes(x)[1]):
                    partial_copy(t, x, e, k).wait_send()

    @pl.loop(0, species)
    def _(i):
        @pl.loop(0, pieces)
        def _(k):
            face_copy(i, 0, k).wait_send()
            face_copy(i, 1, k).wait_send()

        for x in range(cells):
            @pl.when(odd)
            def _():
                below_copy(i, x).wait_send()

            @pl.when((mom % 2 == 0) & (mom > 0))
            def _():
                h_copy(i, x, 0).wait_send()
                h_copy(i, x, 1).wait_send()


def place_kernel(done, parent_ref, out_hbm, out_sem):
    species, cells = out_hbm.shape[1:3]
    order = classes(parent_ref)
    copies = [
        pltpu.make_async_copy(done.at[i * cells + x], out_hbm.at[:, order[i], x], out_sem.at[i, x])
        for i in range(species)
        for x in range(cells)
    ]
    for copy in copies:
        copy.start()
    for copy in copies:
        copy.wait()


def local(
    ny,
    nx,
    which,
    kids,
    spectra,
    production,
    bin_group,
    parent_of,
    diffusivity,
    height_inverse,
    loss_rate,
    density,
):
    bins, species, cells, heights, radii = spectra.shape
    chunks = len(kids) * cells
    block = (bins, heights, radii)
    plane = (heights, radii)
    pieces = heights // ROWS
    split = (pieces, bins, ROWS, radii)
    most = max(nx, ny)
    group = cells * max(1, 256 // (heights * cells))
    dma = pltpu.SemaphoreType.DMA
    tall, broad = ny * bins * ROWS, nx * bins * ROWS
    args = (
        spectra, production, bin_group, parent_of, diffusivity, height_inverse, loss_rate, density
    )
    done = pl.pallas_call(
        functools.partial(step_kernel, ny, nx, kids),
        out_shape=jax.ShapeDtypeStruct((species * cells,) + block, jnp.float32),
        in_specs=[HBM] * len(args),
        out_specs=VMEM,
        scratch_shapes=[
            pltpu.VMEM(spectra.shape, jnp.float32),
            pltpu.SMEM(parent_of.shape, jnp.int32),
            pltpu.SMEM(parent_of.shape, jnp.int32),
            pltpu.SMEM(bin_group.shape, jnp.int32),
            pltpu.VMEM(production.shape, jnp.bfloat16),
            pltpu.VMEM(plane, jnp.float32),
            pltpu.VMEM(height_inverse.shape, jnp.float32),
            pltpu.SMEM(loss_rate.shape, jnp.float32),
            pltpu.VMEM(density.shape, jnp.float32),
            pltpu.VMEM((chunks, most) + split, jnp.bfloat16),
            pltpu.VMEM((chunks, most - 1) + split, jnp.bfloat16),
            pltpu.VMEM((chunks, most - 1) + split, jnp.bfloat16),
            pltpu.VMEM((chunks,) + split, jnp.float32),
            pltpu.VMEM((species, 2) + split, jnp.bfloat16),
            pltpu.VMEM((species, 2) + split, jnp.bfloat16),
            pltpu.VMEM((species, cells) + plane, jnp.float32),
            pltpu.VMEM((species, cells) + plane, jnp.bfloat16),
            pltpu.VMEM((species, cells) + plane, jnp.bfloat16),
            pltpu.VMEM((species, cells) + plane, jnp.bfloat16),
            pltpu.VMEM((cells,) + plane, jnp.float32),
            pltpu.VMEM((species, cells) + plane, jnp.bfloat16),
            pltpu.VMEM((bins, cells) + plane, jnp.float32),
            pltpu.VMEM((2, cells) + plane, jnp.float32),
            pltpu.VMEM((max(bins, 8), radii), jnp.float32),
            pltpu.VMEM((max(bins, 8), radii), jnp.float32),
            pltpu.VMEM((tall, broad), jnp.bfloat16),
            pltpu.VMEM((broad, tall), jnp.bfloat16),
            pltpu.VMEM((2, group * heights, group * heights), jnp.bfloat16),
            pltpu.VMEM((3,) + plane, jnp.float32),
            dma((7,)),
            dma((pieces,)),
            dma((chunks, most - 1, pieces)),
            dma((chunks, most - 1, pieces)),
            dma((chunks, most - 1, pieces)),
            dma((chunks, most - 1, pieces)),
            dma((species, 2, pieces)),
            dma((species, 2, pieces)),
            dma((species, cells)),
            dma((species, cells)),
            dma((species, cells, 2)),
            dma((species, cells)),
            dma,
            dma,
        ],
        compiler_params=pltpu.CompilerParams(
            collective_id=which, has_side_effects=True, vmem_limit_bytes=36 * 1024 * 1024
        ),
    )(*map(stay, args))
    return place(done, parent_of, spectra)


def place(done, parent_of, spectra):
    species, cells = spectra.shape[1:3]
    dma = pltpu.SemaphoreType.DMA
    return pl.pallas_call(
        place_kernel,
        out_shape=pltpu.HBM(spectra.shape, jnp.float32),
        in_specs=[VMEM, pl.BlockSpec(memory_space=pltpu.SMEM)],
        out_specs=HBM,
        scratch_shapes=[dma((species, cells))],
        compiler_params=pltpu.CompilerParams(vmem_limit_bytes=16 * 1024 * 1024),
    )(done, parent_of)


def step(ny, nx, *args):
    parent_of = args[3]
    species = parent_of.shape[0]
    forms = ((1,) * species,)
    if species == 4:
        forms += ((2, 1, 1), (2, 2), (3, 1))
    kernels = [functools.partial(local, ny, nx, n, kids) for n, kids in enumerate(forms)]
    if species == 4:
        later = np.triu(np.ones((species, species), np.bool_), 1)
        same = (parent_of[:, None] == parent_of[None, :]) & later
        return lax.switch(jnp.sum(same.astype(jnp.int32)), kernels, *args)
    return kernels[0](*args)


def solution(mesh):
    ny, nx = grid_of(mesh.shape["mom"])
    return jax.shard_map(
        functools.partial(step, ny, nx),
        mesh=mesh,
        in_specs=(
            P("mom", None, "phi", None, None),
            P(),
            P(),
            P(),
            P(),
            P(),
            P("mom"),
            P("phi", None, None),
        ),
        out_specs=P("mom", None, "phi", None, None),
        check_vma=False,
    )
```

```python
import functools
import math

import jax
import jax.numpy as jnp
import numpy as np
from jax import lax
from jax.experimental import pallas as pl
from jax.experimental.pallas import tpu as pltpu
from jax.sharding import PartitionSpec as P

MESH = pl.DeviceIdType.MESH
ROWS = 16
VMEM = pl.BlockSpec(memory_space=pltpu.VMEM)
HBM = pl.BlockSpec(memory_space=pltpu.HBM)
stay = functools.partial(pltpu.with_memory_space_constraint, memory_space=pltpu.HBM)


def grid_of(count):
    columns = max(d for d in range(1, math.isqrt(count) + 1) if count % d == 0)
    return count // columns, columns


def dot(a, b):
    return jnp.dot(a, b, preferred_element_type=jnp.float32)


def dot_nt(a, b):
    return lax.dot_general(a, b, (((1,), (1,)), ((), ())), preferred_element_type=jnp.float32)


def onehot_bins(first_bins, bins, total):
    local = lax.broadcasted_iota(jnp.int32, (bins, ROWS, total), 0)
    whole = lax.broadcasted_iota(jnp.int32, (bins, ROWS, total), 2)
    parts = [
        jnp.where(local + first == whole, 1.0, 0.0).reshape(bins * ROWS, total)
        for first in first_bins
    ]
    return jnp.concatenate(parts, axis=0).astype(jnp.bfloat16)


def coded(value):
    fourth = (value * value) * (value * value)
    return jnp.where(value < 0.0, -fourth, fourth).astype(jnp.bfloat16)


def decoded(code):
    code = code.astype(jnp.float32)
    root = jnp.sqrt(jnp.sqrt(jnp.abs(code)))
    return jnp.where(code < 0.0, -root, root)


def classes(parent_ref):
    n = parent_ref.shape[0]
    parent = [parent_ref[s] for s in range(n)]
    keys = []
    for s in range(n):
        size, first = 0, n
        for j in range(n - 1, -1, -1):
            equal = parent[j] == parent[s]
            size = size + jnp.where(equal, 1, 0)
            first = jnp.where(equal, j, first)
        keys.append((n - size) * (n * n) + first * n + s)
    ranks = [sum(jnp.where(keys[j] < keys[s], 1, 0) for j in range(n) if j != s) for s in range(n)]
    return [sum(jnp.where(ranks[s] == i, s, 0) for s in range(1, n)) for i in range(n)]


def step_kernel(
    ny,
    nx,
    kids,
    f_hbm,
    production_hbm,
    group_hbm,
    parent_hbm,
    diff_hbm,
    inverse_hbm,
    rate_hbm,
    density_hbm,
    acc,
    f_ref,
    parent_ref,
    order_ref,
    group_ref,
    production_ref,
    diff_ref,
    inverse_ref,
    rate_ref,
    density_ref,
    comb,
    psend,
    precv,
    own_part,
    faces_out,
    faces_in,
    below,
    below_out,
    above,
    entered,
    hin,
    hout,
    weight,
    keep,
    rates_out,
    rates_in,
    wide_0,
    wide_1,
    height,
    coef,
    in_sem,
    f_sem,
    x_send,
    x_recv,
    y_send,
    y_recv,
    f_send,
    f_recv,
    a_send,
    a_recv,
    h_send,
    h_recv,
    r_send,
    r_recv,
):
    bins, species, cells, heights, radii = f_ref.shape
    pieces = heights // ROWS
    total_bins = production_ref.shape[0]
    count = ny * nx
    slots = len(kids)
    per = height.shape[1] // (heights * cells)
    parts = bins // per
    apart = slots == 2 and kids[0] > 1
    wides = (wide_0, wide_1)
    phi = lax.axis_index("phi")
    mom = lax.axis_index("mom")
    phis = lax.axis_size("phi")
    row, col = mom // nx, mom % nx
    right, left = (phi + 1) % phis, (phi + phis - 1) % phis

    def first_of(t):
        return sum(jnp.where(t > j, kids[j], 0) for j in range(slots))

    def rows(k):
        return pl.ds(pl.multiple_of(k * ROWS, ROWS), ROWS)

    small = [
        pltpu.make_async_copy(parent_hbm, parent_ref, in_sem.at[0]),
        pltpu.make_async_copy(group_hbm, group_ref, in_sem.at[1]),
        pltpu.make_async_copy(production_hbm, production_ref, in_sem.at[2]),
        pltpu.make_async_copy(rate_hbm, rate_ref, in_sem.at[3]),
        pltpu.make_async_copy(diff_hbm, diff_ref, in_sem.at[4]),
        pltpu.make_async_copy(inverse_hbm, inverse_ref, in_sem.at[5]),
        pltpu.make_async_copy(density_hbm, density_ref, in_sem.at[6]),
    ]
    loads = [
        pltpu.make_async_copy(
            f_hbm.at[:, :, :, pl.ds(k * ROWS, ROWS), :],
            f_ref.at[:, :, :, pl.ds(k * ROWS, ROWS), :],
            f_sem.at[k],
        )
        for k in range(pieces)
    ]
    small[0].start()
    for copy in loads:
        copy.start()
    for copy in small[1:]:
        copy.start()
    barrier = pltpu.get_barrier_semaphore()
    for d in range(1, count):
        pl.semaphore_signal(
            barrier, inc=1, device_id={"mom": (mom + d) % count}, device_id_type=MESH
        )
    for side in (left, right):
        pl.semaphore_signal(barrier, inc=1, device_id={"phi": side}, device_id_type=MESH)

    def along_row(d):
        return {"mom": row * nx + (col + d) % nx}

    def along_col(e):
        return {"mom": ((row + e) % ny) * nx + col}

    def sizes(x):
        return (nx, ny) if x % 2 == 0 else (ny, nx)

    def parent_copy(t, x, d, k):
        c = t * cells + x
        return pltpu.make_async_remote_copy(
            src_ref=comb.at[c, 0, k],
            dst_ref=comb.at[c, d, k],
            send_sem=x_send.at[c, d - 1, k],
            recv_sem=x_recv.at[c, d - 1, k],
            device_id=along_row(d) if x % 2 == 0 else along_col(d),
            device_id_type=MESH,
        )

    def some(b):
        return pl.ds(b * per, per)

    def partial_copy(t, x, e, b):
        c = t * cells + x
        return pltpu.make_async_remote_copy(
            src_ref=psend.at[c, e - 1, some(b)],
            dst_ref=precv.at[c, e - 1, some(b)],
            send_sem=y_send.at[c, e - 1, b],
            recv_sem=y_recv.at[c, e - 1, b],
            device_id=along_col(e) if x % 2 == 0 else along_row(e),
            device_id_type=MESH,
        )

    def face_copy(i, side, b):
        return pltpu.make_async_remote_copy(
            src_ref=faces_out.at[i, side, some(b)],
            dst_ref=faces_in.at[i, side, some(b)],
            send_sem=f_send.at[i, side, b],
            recv_sem=f_recv.at[i, side, b],
            device_id={"phi": left if side == 0 else right},
            device_id_type=MESH,
        )

    def below_copy(i, x):
        return pltpu.make_async_remote_copy(
            src_ref=below_out.at[i, x],
            dst_ref=above.at[i, x],
            send_sem=a_send.at[i, x],
            recv_sem=a_recv.at[i, x],
            device_id={"mom": (mom + count - 1) % count},
            device_id_type=MESH,
        )

    def h_copy(i, x, n):
        return pltpu.make_async_remote_copy(
            src_ref=hout.at[i, x],
            dst_ref=entered.at[i, x],
            send_sem=h_send.at[i, x, n],
            recv_sem=h_recv.at[i, x],
            device_id={"mom": (mom + count - 1 - n) % count},
            device_id_type=MESH,
        )

    def rate_copy():
        return pltpu.make_async_remote_copy(
            src_ref=rates_out,
            dst_ref=rates_in,
            send_sem=r_send,
            recv_sem=r_recv,
            device_id={"mom": (mom + count - 1) % count},
            device_id_type=MESH,
        )

    def send_parents(t, k):
        for x in range(cells):
            for d in range(1, sizes(x)[0]):
                parent_copy(t, x, d, k).start()

    odd = mom % 2 == 1
    ahead = 2
    small[0].wait()
    for i, s in enumerate(classes(parent_ref)):
        order_ref[i] = s
    parent = parent_ref[order_ref[0]]
    for k in range(pieces):
        loads[k].wait()
        at = pl.ds(k * ROWS, ROWS)
        for x in range(cells):
            chosen = f_ref[:, 0, x, at, :]
            for s in range(1, species):
                chosen = jnp.where(parent == s, f_ref[:, s, x, at, :], chosen)
            comb[x, 0, k] = chosen.astype(jnp.bfloat16)
        if k == 0:
            pl.semaphore_wait(barrier, count + 1)
        send_parents(0, k)

    @pl.loop(1, slots)
    def _(t):
        parent = parent_ref[order_ref[first_of(t)]]

        @pl.loop(0, pieces)
        def _(k):
            for x in range(cells):
                comb[t * cells + x, 0, k] = f_ref[:, parent, x, rows(k), :].astype(jnp.bfloat16)

            @pl.when(t < ahead)
            def _():
                send_parents(t, k)

    if apart:
        @pl.loop(0, kids[0])
        def _(i):
            @pl.loop(0, parts)
            def _(b):
                for side, x in enumerate((0, cells - 1)):
                    face = f_ref[some(b), order_ref[i], x]
                    faces_out[i, side, some(b)] = face.astype(jnp.bfloat16)
                    face_copy(i, side, b).start()

    below[...] = jnp.zeros_like(below)
    for copy in small[1:]:
        copy.wait()
    for p in range(bins):
        rates_out[pl.ds(p, 1), :] = jnp.full((1, radii), rate_ref[p], jnp.float32)

    @pl.when(odd)
    def _():
        rate_copy().start()

    p_at = lax.broadcasted_iota(jnp.int32, (total_bins, total_bins), 0)
    q_at = lax.broadcasted_iota(jnp.int32, (total_bins, total_bins), 1)
    p_group = jnp.zeros((total_bins, total_bins), jnp.int32)
    q_group = jnp.zeros((total_bins, total_bins), jnp.int32)
    for b in range(total_bins):
        p_group = jnp.where(p_at == b, group_ref[b], p_group)
        q_group = jnp.where(q_at == b, group_ref[b], q_group)
    kernel = jnp.where(p_group == q_group, production_ref[...].astype(jnp.float32), 0.0)
    kernel = kernel.astype(jnp.bfloat16)
    row_starts = [(row * nx + (col + d) % nx) * bins for d in range(nx)]
    col_starts = [(((row + e) % ny) * nx + col) * bins for e in range(ny)]
    row_froms = [(row * nx + (col + nx - d) % nx) * bins for d in range(nx)]
    col_froms = [(((row + ny - e) % ny) * nx + col) * bins for e in range(ny)]
    for to, source_from, ref in ((col_starts, row_froms, wide_0), (row_starts, col_froms, wide_1)):
        rows_1h = onehot_bins(to, bins, total_bins)
        cols_1h = onehot_bins(source_from, bins, total_bins)
        mixed = dot_nt(dot(rows_1h, kernel).astype(jnp.bfloat16), cols_1h)
        r_at = lax.broadcasted_iota(jnp.int32, mixed.shape, 0) & (ROWS - 1)
        c_at = lax.broadcasted_iota(jnp.int32, mixed.shape, 1) & (ROWS - 1)
        ref[...] = jnp.where(r_at == c_at, mixed, 0.0).astype(jnp.bfloat16)

    group = height.shape[1] // heights
    a_at = lax.broadcasted_iota(jnp.int32, (heights, heights), 0)
    b_at = lax.broadcasted_iota(jnp.int32, (heights, heights), 1)
    stencil = jnp.where(a_at == b_at, 0.5, 0.0) + jnp.where(jnp.abs(a_at - b_at) == 1, 0.25, 0.0)
    both = jnp.dot(
        inverse_ref[...],
        stencil,
        precision=lax.Precision.HIGHEST,
        preferred_element_type=jnp.float32,
    )
    high = both.astype(jnp.bfloat16).astype(jnp.float32)
    tall_a = lax.broadcasted_iota(jnp.int32, (group, heights, heights), 1)
    tall_b = lax.broadcasted_iota(jnp.int32, (group, heights, heights), 2)
    spread = jnp.where(tall_a == tall_b, 1.0, 0.0).reshape(group * heights, heights)
    spread = spread.astype(jnp.bfloat16)
    row_g = lax.broadcasted_iota(jnp.int32, (group, heights, group * heights), 0)
    col_g = lax.broadcasted_iota(jnp.int32, (group, heights, group * heights), 2)
    first = row_g * heights
    inside = jnp.where((col_g >= first) & (col_g < first + heights), 1.0, 0.0)
    inside = inside.reshape(group * heights, group * heights)
    for n, part in enumerate((high, both - high)):
        tall = jnp.concatenate([part] * group, axis=0).astype(jnp.bfloat16)
        height[n] = (dot_nt(tall, spread) * inside).astype(jnp.bfloat16)

    diff = diff_ref[...]
    lane = lax.broadcasted_iota(jnp.int32, diff.shape, 1)
    coef[0] = 1.0 - 3.0 * diff
    coef[1] = jnp.where(lane == 0, 0.0, 0.5 * diff)
    coef[2] = jnp.where(lane == radii - 1, 0.0, 0.5 * diff)

    for x in range(cells):
        @pl.loop(0, pieces)
        def _(k):
            kept = jnp.ones((ROWS, radii), jnp.float32)
            for p in range(bins):
                part = 1.0 / (1.0 + 0.5 * rate_ref[p] * density_ref[x, rows(k), :])
                weight[p, x, rows(k), :] = part
                kept = kept * (1.0 - part)
            keep[0, x, rows(k), :] = kept

    def keep_above():
        rate_copy().wait_recv()
        for x in range(cells):
            @pl.loop(0, pieces)
            def _(k):
                dens = density_ref[x, rows(k), :]
                kept = jnp.ones((ROWS, radii), jnp.float32)
                for p in range(bins):
                    kept = kept * (1.0 - 1.0 / (1.0 + 0.5 * rates_in[pl.ds(p, 1), :] * dens))
                keep[1, x, rows(k), :] = kept

    @pl.when(mom >= count - 2)
    def _():
        entered[...] = jnp.zeros_like(entered)

    def mix(t):
        @pl.loop(0, pieces)
        def _(k):
            for x in range(cells):
                c = t * cells + x
                n1, n2 = sizes(x)
                for d in range(1, n1):
                    parent_copy(t, x, d, k).wait_recv()
                block = comb[c, :n1, k].reshape(n1 * bins * ROWS, radii)
                sums = dot(wides[x % 2][...], block).reshape(n2, bins, ROWS, radii)
                own_part[c, :, rows(k), :] = sums[0]
                for e in range(1, n2):
                    psend[c, e - 1, :, rows(k), :] = sums[e].astype(jnp.bfloat16)

        @pl.loop(0, parts)
        def _(n):
            for x in range(cells):
                for e in range(1, sizes(x)[1]):
                    partial_copy(t, x, e, parts - 1 - n).start()

        @pl.when(t + ahead < slots)
        def _():
            @pl.loop(0, pieces)
            def _(k):
                send_parents(t + ahead, k)

    def source(t, b):
        for x in range(cells):
            c = t * cells + x
            n2 = sizes(x)[1]
            for e in range(1, n2):
                partial_copy(t, x, e, b).wait_recv()

            def send_face(i, value):
                rounded = value.astype(jnp.bfloat16)
                for side, face in enumerate((0, cells - 1)):
                    if x == face:
                        faces_out[i, side, some(b)] = rounded
                        face_copy(i, side, b).start()

            def gained():
                value = own_part[c, some(b)]
                for e in range(1, n2):
                    value = value + precv[c, e - 1, some(b)].astype(jnp.float32)
                return value

            if apart:
                @pl.when(t == 0)
                def _():
                    send_face(species, gained())

            @pl.loop(first_of(t), first_of(t + 1))
            def _(i):
                total = f_ref[some(b), order_ref[i], x] + gained()
                acc[i * cells + x, some(b)] = total
                if apart:
                    @pl.when(t > 0)
                    def _():
                        send_face(i, total)
                else:
                    send_face(i, total)

    def diffuse(i):
        first = i * cells

        @pl.loop(0, parts)
        def _(n):
            b = parts - 1 - n
            for side in range(2):
                face_copy(i, side, b).wait_recv()
            if apart:
                @pl.when(i == 0)
                def _():
                    for side in range(2):
                        face_copy(species, side, b).wait_recv()

            planes = []
            for j in range(per):
                p = b * per + j
                own = [acc[first + x, p] for x in range(cells)]
                ends = [faces_in[i, side, p].astype(jnp.float32) for side in range(2)]
                if apart:
                    ends = [
                        end + jnp.where(i < kids[0], faces_in[species, side, p].astype(jnp.float32), 0.0)
                        for side, end in enumerate(ends)
                    ]
                before = [ends[1]] + own[:-1]
                after = own[1:] + [ends[0]]
                for x in range(cells):
                    moved = coef[0] * own[x] + diff_ref[...] * (before[x] + after[x])
                    moved += coef[1] * pltpu.roll(own[x], 1, 1)
                    moved += coef[2] * pltpu.roll(own[x], radii - 1, 1)
                    planes.append(moved)
            moved = jnp.concatenate(planes, axis=0)
            high = moved.astype(jnp.bfloat16)
            low = (moved - high.astype(jnp.float32)).astype(jnp.bfloat16)
            settled = dot(height[0], high) + dot(height[0], low) + dot(height[1], high)
            for x in range(cells):
                carry = below[i, x]
                for j in range(per - 1, -1, -1):
                    m = j * cells + x
                    part = settled[m * heights : (m + 1) * heights]
                    acc[first + x, b * per + j] = part
                    total = 2.0 * part + carry
                    carry = total - total * weight[b * per + j, x]
                below[i, x] = carry

        for x in range(cells):
            below_out[i, x] = coded(below[i, x])

    def send_below(i):
        @pl.when(odd)
        def _():
            for x in range(cells):
                below_copy(i, x).start()

    def finish(i):
        span = heights // 2
        for x in range(cells):
            @pl.when(odd)
            def _():
                @pl.when(mom < count - 1)
                def _():
                    h_copy(i, x, 0).wait_recv()

                hin[x] = decoded(entered[i, x])

            @pl.when(mom % 2 == 0)
            def _():
                below_copy(i, x).wait_recv()

                @pl.when(mom < count - 2)
                def _():
                    h_copy(i, x, 1).wait_recv()

                entering = decoded(above[i, x]) + keep[1, x] * decoded(entered[i, x])
                hin[x] = entering
                hout[i, x] = coded(below[i, x] + keep[0, x] * entering)

                @pl.when(mom > 0)
                def _():
                    h_copy(i, x, 0).start()
                    h_copy(i, x, 1).start()

            @pl.loop(0, 2)
            def _(k):
                at = pl.ds(pl.multiple_of(k * span, span), span)
                carry = hin[x, at, :]
                for p in range(bins - 1, -1, -1):
                    settled = acc[i * cells + x, p, at, :]
                    total = 2.0 * settled + carry
                    both = total * weight[p, x, at, :]
                    acc[i * cells + x, p, at, :] = both - settled
                    carry = total - both

    early = species - kids[-1]

    @pl.loop(0, slots + 2)
    def _(i):
        @pl.when(i < slots)
        def _():
            mix(i)

        @pl.when(i == slots - 1)
        def _():
            @pl.when(mom % 2 == 0)
            def _():
                keep_above()

            @pl.loop(0, sum(kids[: max(slots - 3, 0)]))
            def _(j):
                send_below(j)

        @pl.when((i == slots + 1) & (mom == count - 2))
        def _():
            @pl.loop(0, early)
            def _(j):
                finish(j)

        @pl.when((i >= 1) & (i < slots + 1))
        def _():
            @pl.loop(0, parts)
            def _(n):
                source(i - 1, parts - 1 - n)

        @pl.when(i >= 2)
        def _():
            @pl.loop(first_of(i - 2), first_of(i - 1))
            def _(j):
                diffuse(j)

                @pl.when(i >= slots - 1)
                def _():
                    send_below(j)

    @pl.loop(jnp.where(mom == count - 2, early, 0), species)
    def _(j):
        finish(j)

    @pl.when(odd)
    def _():
        rate_copy().wait_send()

    @pl.loop(0, slots)
    def _(t):
        @pl.loop(0, pieces)
        def _(k):
            for x in range(cells):
                for d in range(1, sizes(x)[0]):
                    parent_copy(t, x, d, k).wait_send()

        @pl.loop(0, parts)
        def _(b):
            for x in range(cells):
                for e in range(1, sizes(x)[1]):
                    partial_copy(t, x, e, b).wait_send()

    @pl.loop(0, species + int(apart))
    def _(i):
        @pl.loop(0, parts)
        def _(b):
            face_copy(i, 0, b).wait_send()
            face_copy(i, 1, b).wait_send()

    @pl.loop(0, species)
    def _(i):
        for x in range(cells):
            @pl.when(odd)
            def _():
                below_copy(i, x).wait_send()

            @pl.when((mom % 2 == 0) & (mom > 0))
            def _():
                h_copy(i, x, 0).wait_send()
                h_copy(i, x, 1).wait_send()


def place_kernel(done, parent_ref, out_hbm, out_sem):
    species, cells = out_hbm.shape[1:3]
    order = classes(parent_ref)
    copies = [
        pltpu.make_async_copy(done.at[i * cells + x], out_hbm.at[:, order[i], x], out_sem.at[i, x])
        for i in range(species)
        for x in range(cells)
    ]
    for copy in copies:
        copy.start()
    for copy in copies:
        copy.wait()


def local(
    ny,
    nx,
    which,
    kids,
    spectra,
    production,
    bin_group,
    parent_of,
    diffusivity,
    height_inverse,
    loss_rate,
    density,
):
    bins, species, cells, heights, radii = spectra.shape
    chunks = len(kids) * cells
    block = (bins, heights, radii)
    plane = (heights, radii)
    pieces = heights // ROWS
    split = (pieces, bins, ROWS, radii)
    most = max(nx, ny)
    group = cells * max(1, 256 // (heights * cells))
    parts = bins * cells // group
    dma = pltpu.SemaphoreType.DMA
    tall, broad = ny * bins * ROWS, nx * bins * ROWS
    args = (
        spectra, production, bin_group, parent_of, diffusivity, height_inverse, loss_rate, density
    )
    done = pl.pallas_call(
        functools.partial(step_kernel, ny, nx, kids),
        out_shape=jax.ShapeDtypeStruct((species * cells,) + block, jnp.float32),
        in_specs=[HBM] * len(args),
        out_specs=VMEM,
        scratch_shapes=[
            pltpu.VMEM(spectra.shape, jnp.float32),
            pltpu.SMEM(parent_of.shape, jnp.int32),
            pltpu.SMEM(parent_of.shape, jnp.int32),
            pltpu.SMEM(bin_group.shape, jnp.int32),
            pltpu.VMEM(production.shape, jnp.bfloat16),
            pltpu.VMEM(plane, jnp.float32),
            pltpu.VMEM(height_inverse.shape, jnp.float32),
            pltpu.SMEM(loss_rate.shape, jnp.float32),
            pltpu.VMEM(density.shape, jnp.float32),
            pltpu.VMEM((chunks, most) + split, jnp.bfloat16),
            pltpu.VMEM((chunks, most - 1) + block, jnp.bfloat16),
            pltpu.VMEM((chunks, most - 1) + block, jnp.bfloat16),
            pltpu.VMEM((chunks,) + block, jnp.float32),
            pltpu.VMEM((species + 1, 2) + block, jnp.bfloat16),
            pltpu.VMEM((species + 1, 2) + block, jnp.bfloat16),
            pltpu.VMEM((species, cells) + plane, jnp.float32),
            pltpu.VMEM((species, cells) + plane, jnp.bfloat16),
            pltpu.VMEM((species, cells) + plane, jnp.bfloat16),
            pltpu.VMEM((species, cells) + plane, jnp.bfloat16),
            pltpu.VMEM((cells,) + plane, jnp.float32),
            pltpu.VMEM((species, cells) + plane, jnp.bfloat16),
            pltpu.VMEM((bins, cells) + plane, jnp.float32),
            pltpu.VMEM((2, cells) + plane, jnp.float32),
            pltpu.VMEM((max(bins, 8), radii), jnp.float32),
            pltpu.VMEM((max(bins, 8), radii), jnp.float32),
            pltpu.VMEM((tall, broad), jnp.bfloat16),
            pltpu.VMEM((broad, tall), jnp.bfloat16),
            pltpu.VMEM((2, group * heights, group * heights), jnp.bfloat16),
            pltpu.VMEM((3,) + plane, jnp.float32),
            dma((7,)),
            dma((pieces,)),
            dma((chunks, most - 1, pieces)),
            dma((chunks, most - 1, pieces)),
            dma((chunks, most - 1, parts)),
            dma((chunks, most - 1, parts)),
            dma((species + 1, 2, parts)),
            dma((species + 1, 2, parts)),
            dma((species, cells)),
            dma((species, cells)),
            dma((species, cells, 2)),
            dma((species, cells)),
            dma,
            dma,
        ],
        compiler_params=pltpu.CompilerParams(
            collective_id=which, has_side_effects=True, vmem_limit_bytes=36 * 1024 * 1024
        ),
    )(*map(stay, args))
    return place(done, parent_of, spectra)


def place(done, parent_of, spectra):
    species, cells = spectra.shape[1:3]
    dma = pltpu.SemaphoreType.DMA
    return pl.pallas_call(
        place_kernel,
        out_shape=pltpu.HBM(spectra.shape, jnp.float32),
        in_specs=[VMEM, pl.BlockSpec(memory_space=pltpu.SMEM)],
        out_specs=HBM,
        scratch_shapes=[dma((species, cells))],
        compiler_params=pltpu.CompilerParams(vmem_limit_bytes=16 * 1024 * 1024),
    )(done, parent_of)


def step(ny, nx, *args):
    parent_of = args[3]
    species = parent_of.shape[0]
    forms = ((1,) * species,)
    if species == 4:
        forms += ((2, 1, 1), (2, 2), (3, 1))
    kernels = [functools.partial(local, ny, nx, n, kids) for n, kids in enumerate(forms)]
    if species == 4:
        later = np.triu(np.ones((species, species), np.bool_), 1)
        same = (parent_of[:, None] == parent_of[None, :]) & later
        return lax.switch(jnp.sum(same.astype(jnp.int32)), kernels, *args)
    return kernels[0](*args)


def solution(mesh):
    ny, nx = grid_of(mesh.shape["mom"])
    return jax.shard_map(
        functools.partial(step, ny, nx),
        mesh=mesh,
        in_specs=(
            P("mom", None, "phi", None, None),
            P(),
            P(),
            P(),
            P(),
            P(),
            P("mom"),
            P("phi", None, None),
        ),
        out_specs=P("mom", None, "phi", None, None),
        check_vma=False,
    )
```

```python
import functools
import math

import jax
import jax.numpy as jnp
from jax import lax
from jax.experimental import pallas as pl
from jax.experimental.pallas import tpu as pltpu
from jax.sharding import PartitionSpec as P

MESH = pl.DeviceIdType.MESH
ROWS = 16
VMEM = pl.BlockSpec(memory_space=pltpu.VMEM)
SMEM = pl.BlockSpec(memory_space=pltpu.SMEM)
HBM = pl.BlockSpec(memory_space=pltpu.HBM)
stay = functools.partial(pltpu.with_memory_space_constraint, memory_space=pltpu.HBM)


def grid_of(count):
    columns = max(d for d in range(1, math.isqrt(count) + 1) if count % d == 0)
    return count // columns, columns


def dot(a, b):
    return jnp.dot(a, b, preferred_element_type=jnp.float32)


def dot_nt(a, b):
    return lax.dot_general(a, b, (((1,), (1,)), ((), ())), preferred_element_type=jnp.float32)


def onehot_bins(first_bins, bins, total):
    local = lax.broadcasted_iota(jnp.int32, (bins, ROWS, total), 0)
    whole = lax.broadcasted_iota(jnp.int32, (bins, ROWS, total), 2)
    parts = [
        jnp.where(local + first == whole, 1.0, 0.0).reshape(bins * ROWS, total)
        for first in first_bins
    ]
    return jnp.concatenate(parts, axis=0).astype(jnp.bfloat16)


def coded(value):
    fourth = (value * value) * (value * value)
    return jnp.where(value < 0.0, -fourth, fourth).astype(jnp.bfloat16)


def decoded(code):
    code = code.astype(jnp.float32)
    root = jnp.sqrt(jnp.sqrt(jnp.abs(code)))
    return jnp.where(code < 0.0, -root, root)


def classes(parent):
    n = len(parent)
    keys = []
    for s in range(n):
        size, first = 0, n
        for j in range(n - 1, -1, -1):
            equal = parent[j] == parent[s]
            size = size + jnp.where(equal, 1, 0)
            first = jnp.where(equal, j, first)
        keys.append((n - size) * (n * n) + first * n + s)
    ranks = [sum(jnp.where(keys[j] < keys[s], 1, 0) for j in range(n) if j != s) for s in range(n)]
    return [sum(jnp.where(ranks[s] == i, s, 0) for s in range(1, n)) for i in range(n)]


def step_kernel(
    ny,
    nx,
    kids,
    f_hbm,
    production_hbm,
    group_hbm,
    parent_hbm,
    diff_hbm,
    inverse_hbm,
    rate_hbm,
    density_hbm,
    acc,
    f_ref,
    parent_ref,
    order_ref,
    group_ref,
    production_ref,
    diff_ref,
    inverse_ref,
    rate_ref,
    density_ref,
    comb,
    psend,
    precv,
    own_part,
    faces_out,
    faces_in,
    below,
    below_out,
    above,
    entered,
    hin,
    hout,
    weight,
    keep,
    rates_out,
    rates_in,
    wide_0,
    wide_1,
    height,
    coef,
    in_sem,
    f_sem,
    x_send,
    x_recv,
    y_send,
    y_recv,
    f_send,
    f_recv,
    a_send,
    a_recv,
    h_send,
    h_recv,
    r_send,
    r_recv,
):
    bins, species, cells, heights, radii = f_ref.shape
    pieces = heights // ROWS
    total_bins = production_ref.shape[0]
    count = ny * nx
    slots = len(kids)
    per = height.shape[1] // (heights * cells)
    parts = bins // per
    apart = slots == 2 and kids[0] > 1
    wides = (wide_0, wide_1)
    phi = lax.axis_index("phi")
    mom = lax.axis_index("mom")
    phis = lax.axis_size("phi")
    row, col = mom // nx, mom % nx
    right, left = (phi + 1) % phis, (phi + phis - 1) % phis

    def first_of(t):
        return sum(jnp.where(t > j, kids[j], 0) for j in range(slots))

    def rows(k):
        return pl.ds(pl.multiple_of(k * ROWS, ROWS), ROWS)

    small = [
        pltpu.make_async_copy(parent_hbm, parent_ref, in_sem.at[0]),
        pltpu.make_async_copy(group_hbm, group_ref, in_sem.at[1]),
        pltpu.make_async_copy(production_hbm, production_ref, in_sem.at[2]),
        pltpu.make_async_copy(rate_hbm, rate_ref, in_sem.at[3]),
        pltpu.make_async_copy(diff_hbm, diff_ref, in_sem.at[4]),
        pltpu.make_async_copy(inverse_hbm, inverse_ref, in_sem.at[5]),
        pltpu.make_async_copy(density_hbm, density_ref, in_sem.at[6]),
    ]
    loads = [
        pltpu.make_async_copy(
            f_hbm.at[:, :, :, pl.ds(k * ROWS, ROWS), :],
            f_ref.at[:, :, :, pl.ds(k * ROWS, ROWS), :],
            f_sem.at[k],
        )
        for k in range(pieces)
    ]
    loads[0].start()
    small[0].start()
    barrier = pltpu.get_barrier_semaphore()
    for d in range(1, count):
        pl.semaphore_signal(
            barrier, inc=1, device_id={"mom": (mom + d) % count}, device_id_type=MESH
        )
    for side in (left, right):
        pl.semaphore_signal(barrier, inc=1, device_id={"phi": side}, device_id_type=MESH)

    def along_row(d):
        return {"mom": row * nx + (col + d) % nx}

    def along_col(e):
        return {"mom": ((row + e) % ny) * nx + col}

    def sizes(x):
        return (nx, ny) if x % 2 == 0 else (ny, nx)

    def parent_copy(t, x, d, k):
        c = t * cells + x
        return pltpu.make_async_remote_copy(
            src_ref=comb.at[c, 0, k],
            dst_ref=comb.at[c, d, k],
            send_sem=x_send.at[c, d - 1, k],
            recv_sem=x_recv.at[c, d - 1, k],
            device_id=along_row(d) if x % 2 == 0 else along_col(d),
            device_id_type=MESH,
        )

    def some(b):
        return pl.ds(b * per, per)

    def partial_copy(t, x, e, b):
        c = t * cells + x
        return pltpu.make_async_remote_copy(
            src_ref=psend.at[c, e - 1, some(b)],
            dst_ref=precv.at[c, e - 1, some(b)],
            send_sem=y_send.at[c, e - 1, b],
            recv_sem=y_recv.at[c, e - 1, b],
            device_id=along_col(e) if x % 2 == 0 else along_row(e),
            device_id_type=MESH,
        )

    def face_copy(i, side, b):
        return pltpu.make_async_remote_copy(
            src_ref=faces_out.at[i, side, some(b)],
            dst_ref=faces_in.at[i, side, some(b)],
            send_sem=f_send.at[i, side, b],
            recv_sem=f_recv.at[i, side, b],
            device_id={"phi": left if side == 0 else right},
            device_id_type=MESH,
        )

    def below_copy(i, x):
        return pltpu.make_async_remote_copy(
            src_ref=below_out.at[i, x],
            dst_ref=above.at[i, x],
            send_sem=a_send.at[i, x],
            recv_sem=a_recv.at[i, x],
            device_id={"mom": (mom + count - 1) % count},
            device_id_type=MESH,
        )

    def h_copy(i, x, n):
        return pltpu.make_async_remote_copy(
            src_ref=hout.at[i, x],
            dst_ref=entered.at[i, x],
            send_sem=h_send.at[i, x, n],
            recv_sem=h_recv.at[i, x],
            device_id={"mom": (mom + count - 1 - n) % count},
            device_id_type=MESH,
        )

    def rate_copy():
        return pltpu.make_async_remote_copy(
            src_ref=rates_out,
            dst_ref=rates_in,
            send_sem=r_send,
            recv_sem=r_recv,
            device_id={"mom": (mom + count - 1) % count},
            device_id_type=MESH,
        )

    def send_parents(t, k):
        for x in range(cells):
            for d in range(1, sizes(x)[0]):
                parent_copy(t, x, d, k).start()

    for copy in loads[1:] + small[1:]:
        copy.start()
    odd = mom % 2 == 1
    ahead = 2
    small[0].wait()
    for i, s in enumerate(classes([parent_ref[s] for s in range(species)])):
        order_ref[i] = s
    parent = parent_ref[order_ref[0]]
    for k in range(pieces):
        loads[k].wait()
        at = pl.ds(k * ROWS, ROWS)
        for x in range(cells):
            chosen = f_ref[:, 0, x, at, :]
            for s in range(1, species):
                chosen = jnp.where(parent == s, f_ref[:, s, x, at, :], chosen)
            comb[x, 0, k] = chosen.astype(jnp.bfloat16)
        if k == 0:
            pl.semaphore_wait(barrier, count + 1)
        send_parents(0, k)

    @pl.loop(1, slots)
    def _(t):
        parent = parent_ref[order_ref[first_of(t)]]

        @pl.loop(0, pieces)
        def _(k):
            for x in range(cells):
                comb[t * cells + x, 0, k] = f_ref[:, parent, x, rows(k), :].astype(jnp.bfloat16)

            @pl.when(t < ahead)
            def _():
                send_parents(t, k)

    if apart:
        @pl.loop(0, kids[0])
        def _(i):
            @pl.loop(0, parts)
            def _(b):
                for side, x in enumerate((0, cells - 1)):
                    face = f_ref[some(b), order_ref[i], x]
                    faces_out[i, side, some(b)] = face.astype(jnp.bfloat16)
                    face_copy(i, side, b).start()

    below[...] = jnp.zeros_like(below)
    for copy in small[1:]:
        copy.wait()
    for p in range(bins):
        rates_out[pl.ds(p, 1), :] = jnp.full((1, radii), rate_ref[p], jnp.float32)

    @pl.when(odd)
    def _():
        rate_copy().start()

    p_at = lax.broadcasted_iota(jnp.int32, (total_bins, total_bins), 0)
    q_at = lax.broadcasted_iota(jnp.int32, (total_bins, total_bins), 1)
    p_group = jnp.zeros((total_bins, total_bins), jnp.int32)
    q_group = jnp.zeros((total_bins, total_bins), jnp.int32)
    for b in range(total_bins):
        p_group = jnp.where(p_at == b, group_ref[b], p_group)
        q_group = jnp.where(q_at == b, group_ref[b], q_group)
    kernel = jnp.where(p_group == q_group, production_ref[...].astype(jnp.float32), 0.0)
    kernel = kernel.astype(jnp.bfloat16)
    row_starts = [(row * nx + (col + d) % nx) * bins for d in range(nx)]
    col_starts = [(((row + e) % ny) * nx + col) * bins for e in range(ny)]
    row_froms = [(row * nx + (col + nx - d) % nx) * bins for d in range(nx)]
    col_froms = [(((row + ny - e) % ny) * nx + col) * bins for e in range(ny)]
    for to, source_from, ref in ((col_starts, row_froms, wide_0), (row_starts, col_froms, wide_1)):
        rows_1h = onehot_bins(to, bins, total_bins)
        cols_1h = onehot_bins(source_from, bins, total_bins)
        mixed = dot_nt(dot(rows_1h, kernel).astype(jnp.bfloat16), cols_1h)
        r_at = lax.broadcasted_iota(jnp.int32, mixed.shape, 0) & (ROWS - 1)
        c_at = lax.broadcasted_iota(jnp.int32, mixed.shape, 1) & (ROWS - 1)
        ref[...] = jnp.where(r_at == c_at, mixed, 0.0).astype(jnp.bfloat16)

    group = height.shape[1] // heights
    a_at = lax.broadcasted_iota(jnp.int32, (heights, heights), 0)
    b_at = lax.broadcasted_iota(jnp.int32, (heights, heights), 1)
    stencil = jnp.where(a_at == b_at, 0.5, 0.0) + jnp.where(jnp.abs(a_at - b_at) == 1, 0.25, 0.0)
    both = jnp.dot(
        inverse_ref[...],
        stencil,
        precision=lax.Precision.HIGHEST,
        preferred_element_type=jnp.float32,
    )
    high = both.astype(jnp.bfloat16).astype(jnp.float32)
    tall_a = lax.broadcasted_iota(jnp.int32, (group, heights, heights), 1)
    tall_b = lax.broadcasted_iota(jnp.int32, (group, heights, heights), 2)
    spread = jnp.where(tall_a == tall_b, 1.0, 0.0).reshape(group * heights, heights)
    spread = spread.astype(jnp.bfloat16)
    row_g = lax.broadcasted_iota(jnp.int32, (group, heights, group * heights), 0)
    col_g = lax.broadcasted_iota(jnp.int32, (group, heights, group * heights), 2)
    first = row_g * heights
    inside = jnp.where((col_g >= first) & (col_g < first + heights), 1.0, 0.0)
    inside = inside.reshape(group * heights, group * heights)
    for n, part in enumerate((high, both - high)):
        tall = jnp.concatenate([part] * group, axis=0).astype(jnp.bfloat16)
        height[n] = (dot_nt(tall, spread) * inside).astype(jnp.bfloat16)

    diff = diff_ref[...]
    lane = lax.broadcasted_iota(jnp.int32, diff.shape, 1)
    coef[0] = 1.0 - 3.0 * diff
    coef[1] = jnp.where(lane == 0, 0.0, 0.5 * diff)
    coef[2] = jnp.where(lane == radii - 1, 0.0, 0.5 * diff)

    for x in range(cells):
        @pl.loop(0, pieces)
        def _(k):
            kept = jnp.ones((ROWS, radii), jnp.float32)
            for p in range(bins):
                part = 1.0 / (1.0 + 0.5 * rate_ref[p] * density_ref[x, rows(k), :])
                weight[p, x, rows(k), :] = part
                kept = kept * (1.0 - part)
            keep[0, x, rows(k), :] = kept

    def keep_above():
        rate_copy().wait_recv()
        for x in range(cells):
            @pl.loop(0, pieces)
            def _(k):
                dens = density_ref[x, rows(k), :]
                kept = jnp.ones((ROWS, radii), jnp.float32)
                for p in range(bins):
                    kept = kept * (1.0 - 1.0 / (1.0 + 0.5 * rates_in[pl.ds(p, 1), :] * dens))
                keep[1, x, rows(k), :] = kept

    @pl.when(mom >= count - 2)
    def _():
        entered[...] = jnp.zeros_like(entered)

    def mix(t):
        @pl.loop(0, pieces)
        def _(k):
            for x in range(cells):
                c = t * cells + x
                n1, n2 = sizes(x)
                for d in range(1, n1):
                    parent_copy(t, x, d, k).wait_recv()
                block = comb[c, :n1, k].reshape(n1 * bins * ROWS, radii)
                sums = dot(wides[x % 2][...], block).reshape(n2, bins, ROWS, radii)
                own_part[c, :, rows(k), :] = sums[0]
                for e in range(1, n2):
                    psend[c, e - 1, :, rows(k), :] = sums[e].astype(jnp.bfloat16)

        @pl.loop(0, parts)
        def _(n):
            for x in range(cells):
                for e in range(1, sizes(x)[1]):
                    partial_copy(t, x, e, parts - 1 - n).start()

        @pl.when(t + ahead < slots)
        def _():
            @pl.loop(0, pieces)
            def _(k):
                send_parents(t + ahead, k)

    def source(t, b):
        for x in range(cells):
            c = t * cells + x
            n2 = sizes(x)[1]
            for e in range(1, n2):
                partial_copy(t, x, e, b).wait_recv()

            def send_face(i, value):
                rounded = value.astype(jnp.bfloat16)
                for side, face in enumerate((0, cells - 1)):
                    if x == face:
                        faces_out[i, side, some(b)] = rounded
                        face_copy(i, side, b).start()

            def gained():
                value = own_part[c, some(b)]
                for e in range(1, n2):
                    value = value + precv[c, e - 1, some(b)].astype(jnp.float32)
                return value

            if apart:
                @pl.when(t == 0)
                def _():
                    send_face(species, gained())

            @pl.loop(first_of(t), first_of(t + 1))
            def _(i):
                total = f_ref[some(b), order_ref[i], x] + gained()
                acc[i * cells + x, some(b)] = total
                if apart:
                    @pl.when(t > 0)
                    def _():
                        send_face(i, total)
                else:
                    send_face(i, total)

    def diffuse(i):
        first = i * cells

        @pl.loop(0, parts)
        def _(n):
            b = parts - 1 - n
            for side in range(2):
                face_copy(i, side, b).wait_recv()
            if apart:
                @pl.when(i == 0)
                def _():
                    for side in range(2):
                        face_copy(species, side, b).wait_recv()

            planes = []
            for j in range(per):
                p = b * per + j
                own = [acc[first + x, p] for x in range(cells)]
                ends = [faces_in[i, side, p].astype(jnp.float32) for side in range(2)]
                if apart:
                    ends = [
                        end + jnp.where(i < kids[0], faces_in[species, side, p].astype(jnp.float32), 0.0)
                        for side, end in enumerate(ends)
                    ]
                before = [ends[1]] + own[:-1]
                after = own[1:] + [ends[0]]
                for x in range(cells):
                    moved = coef[0] * own[x] + diff_ref[...] * (before[x] + after[x])
                    moved += coef[1] * pltpu.roll(own[x], 1, 1)
                    moved += coef[2] * pltpu.roll(own[x], radii - 1, 1)
                    planes.append(moved)
            moved = jnp.concatenate(planes, axis=0)
            high = moved.astype(jnp.bfloat16)
            low = (moved - high.astype(jnp.float32)).astype(jnp.bfloat16)
            settled = dot(height[0], high) + dot(height[0], low) + dot(height[1], high)
            for x in range(cells):
                carry = below[i, x]
                for j in range(per - 1, -1, -1):
                    m = j * cells + x
                    part = settled[m * heights : (m + 1) * heights]
                    acc[first + x, b * per + j] = part
                    total = 2.0 * part + carry
                    carry = total - total * weight[b * per + j, x]
                below[i, x] = carry

        for x in range(cells):
            below_out[i, x] = coded(below[i, x])

    def send_below(i):
        @pl.when(odd)
        def _():
            for x in range(cells):
                below_copy(i, x).start()

    def finish(i):
        span = heights // 2
        for x in range(cells):
            @pl.when(odd)
            def _():
                @pl.when(mom < count - 1)
                def _():
                    h_copy(i, x, 0).wait_recv()

                hin[x] = decoded(entered[i, x])

            @pl.when(mom % 2 == 0)
            def _():
                below_copy(i, x).wait_recv()

                @pl.when(mom < count - 2)
                def _():
                    h_copy(i, x, 1).wait_recv()

                entering = decoded(above[i, x]) + keep[1, x] * decoded(entered[i, x])
                hin[x] = entering
                hout[i, x] = coded(below[i, x] + keep[0, x] * entering)

                @pl.when(mom > 0)
                def _():
                    h_copy(i, x, 0).start()
                    h_copy(i, x, 1).start()

            @pl.loop(0, 2)
            def _(k):
                at = pl.ds(pl.multiple_of(k * span, span), span)
                carry = hin[x, at, :]
                for p in range(bins - 1, -1, -1):
                    settled = acc[i * cells + x, p, at, :]
                    total = 2.0 * settled + carry
                    both = total * weight[p, x, at, :]
                    acc[i * cells + x, p, at, :] = both - settled
                    carry = total - both

    early = species - kids[-1]

    @pl.loop(0, slots + 2)
    def _(i):
        @pl.when(i < slots)
        def _():
            mix(i)

        @pl.when(i == slots - 1)
        def _():
            @pl.when(mom % 2 == 0)
            def _():
                keep_above()

            @pl.loop(0, sum(kids[: max(slots - 3, 0)]))
            def _(j):
                send_below(j)

        @pl.when((i == slots + 1) & (mom == count - 2))
        def _():
            @pl.loop(0, early)
            def _(j):
                finish(j)

        @pl.when((i >= 1) & (i < slots + 1))
        def _():
            @pl.loop(0, parts)
            def _(n):
                source(i - 1, parts - 1 - n)

        @pl.when(i >= 2)
        def _():
            @pl.loop(first_of(i - 2), first_of(i - 1))
            def _(j):
                diffuse(j)

                @pl.when(i >= slots - 1)
                def _():
                    send_below(j)

    @pl.loop(jnp.where(mom == count - 2, early, 0), species)
    def _(j):
        finish(j)

    @pl.when(odd)
    def _():
        rate_copy().wait_send()

    @pl.loop(0, slots)
    def _(t):
        @pl.loop(0, pieces)
        def _(k):
            for x in range(cells):
                for d in range(1, sizes(x)[0]):
                    parent_copy(t, x, d, k).wait_send()

        @pl.loop(0, parts)
        def _(b):
            for x in range(cells):
                for e in range(1, sizes(x)[1]):
                    partial_copy(t, x, e, b).wait_send()

    @pl.loop(0, species + int(apart))
    def _(i):
        @pl.loop(0, parts)
        def _(b):
            face_copy(i, 0, b).wait_send()
            face_copy(i, 1, b).wait_send()

    @pl.loop(0, species)
    def _(i):
        for x in range(cells):
            @pl.when(odd)
            def _():
                below_copy(i, x).wait_send()

            @pl.when((mom % 2 == 0) & (mom > 0))
            def _():
                h_copy(i, x, 0).wait_send()
                h_copy(i, x, 1).wait_send()


def pairs_kernel(parent_ref, pairs_ref):
    n = parent_ref.shape[0]
    pairs_ref[0] = sum(
        jnp.where(parent_ref[a] == parent_ref[b], 1, 0) for a in range(n) for b in range(a)
    )


def place_kernel(done, parent_ref, out_hbm, out_sem):
    species, cells = out_hbm.shape[1:3]
    parent = parent_ref[...]
    order = classes([parent[0, s] for s in range(species)])
    copies = [
        pltpu.make_async_copy(done.at[i * cells + x], out_hbm.at[:, order[i], x], out_sem.at[i, x])
        for i in range(species)
        for x in range(cells)
    ]
    for copy in copies:
        copy.start()
    for copy in copies:
        copy.wait()


def local(
    ny,
    nx,
    which,
    kids,
    spectra,
    production,
    bin_group,
    parent_of,
    diffusivity,
    height_inverse,
    loss_rate,
    density,
):
    bins, species, cells, heights, radii = spectra.shape
    chunks = len(kids) * cells
    block = (bins, heights, radii)
    plane = (heights, radii)
    pieces = heights // ROWS
    split = (pieces, bins, ROWS, radii)
    most = max(nx, ny)
    group = cells * max(1, 256 // (heights * cells))
    parts = bins * cells // group
    dma = pltpu.SemaphoreType.DMA
    tall, broad = ny * bins * ROWS, nx * bins * ROWS
    args = (
        spectra, production, bin_group, parent_of, diffusivity, height_inverse, loss_rate, density
    )
    done = pl.pallas_call(
        functools.partial(step_kernel, ny, nx, kids),
        out_shape=jax.ShapeDtypeStruct((species * cells,) + block, jnp.float32),
        in_specs=[HBM] * len(args),
        out_specs=VMEM,
        scratch_shapes=[
            pltpu.VMEM(spectra.shape, jnp.float32),
            pltpu.SMEM(parent_of.shape, jnp.int32),
            pltpu.SMEM(parent_of.shape, jnp.int32),
            pltpu.SMEM(bin_group.shape, jnp.int32),
            pltpu.VMEM(production.shape, jnp.bfloat16),
            pltpu.VMEM(plane, jnp.float32),
            pltpu.VMEM(height_inverse.shape, jnp.float32),
            pltpu.SMEM(loss_rate.shape, jnp.float32),
            pltpu.VMEM(density.shape, jnp.float32),
            pltpu.VMEM((chunks, most) + split, jnp.bfloat16),
            pltpu.VMEM((chunks, most - 1) + block, jnp.bfloat16),
            pltpu.VMEM((chunks, most - 1) + block, jnp.bfloat16),
            pltpu.VMEM((chunks,) + block, jnp.float32),
            pltpu.VMEM((species + 1, 2) + block, jnp.bfloat16),
            pltpu.VMEM((species + 1, 2) + block, jnp.bfloat16),
            pltpu.VMEM((species, cells) + plane, jnp.float32),
            pltpu.VMEM((species, cells) + plane, jnp.bfloat16),
            pltpu.VMEM((species, cells) + plane, jnp.bfloat16),
            pltpu.VMEM((species, cells) + plane, jnp.bfloat16),
            pltpu.VMEM((cells,) + plane, jnp.float32),
            pltpu.VMEM((species, cells) + plane, jnp.bfloat16),
            pltpu.VMEM((bins, cells) + plane, jnp.float32),
            pltpu.VMEM((2, cells) + plane, jnp.float32),
            pltpu.VMEM((max(bins, 8), radii), jnp.float32),
            pltpu.VMEM((max(bins, 8), radii), jnp.float32),
            pltpu.VMEM((tall, broad), jnp.bfloat16),
            pltpu.VMEM((broad, tall), jnp.bfloat16),
            pltpu.VMEM((2, group * heights, group * heights), jnp.bfloat16),
            pltpu.VMEM((3,) + plane, jnp.float32),
            dma((7,)),
            dma((pieces,)),
            dma((chunks, most - 1, pieces)),
            dma((chunks, most - 1, pieces)),
            dma((chunks, most - 1, parts)),
            dma((chunks, most - 1, parts)),
            dma((species + 1, 2, parts)),
            dma((species + 1, 2, parts)),
            dma((species, cells)),
            dma((species, cells)),
            dma((species, cells, 2)),
            dma((species, cells)),
            dma,
            dma,
        ],
        compiler_params=pltpu.CompilerParams(
            collective_id=which, has_side_effects=True, vmem_limit_bytes=36 * 1024 * 1024
        ),
    )(*map(stay, args))
    return place(done, parent_of, spectra)


def place(done, parent_of, spectra):
    species, cells = spectra.shape[1:3]
    dma = pltpu.SemaphoreType.DMA
    return pl.pallas_call(
        place_kernel,
        out_shape=pltpu.HBM(spectra.shape, jnp.float32),
        in_specs=[VMEM, VMEM],
        out_specs=HBM,
        scratch_shapes=[dma((species, cells))],
        compiler_params=pltpu.CompilerParams(vmem_limit_bytes=16 * 1024 * 1024),
    )(done, parent_of.reshape(1, species))


def step(ny, nx, *args):
    parent_of = args[3]
    species = parent_of.shape[0]
    forms = ((1,) * species,)
    if species == 4:
        forms += ((2, 1, 1), (2, 2), (3, 1))
    kernels = [functools.partial(local, ny, nx, n, kids) for n, kids in enumerate(forms)]
    if species == 4:
        pairs = pl.pallas_call(
            pairs_kernel,
            out_shape=jax.ShapeDtypeStruct((1,), jnp.int32),
            in_specs=[SMEM],
            out_specs=SMEM,
        )(parent_of)
        return lax.switch(pairs[0], kernels, *args)
    return kernels[0](*args)


def solution(mesh):
    ny, nx = grid_of(mesh.shape["mom"])
    return jax.shard_map(
        functools.partial(step, ny, nx),
        mesh=mesh,
        in_specs=(
            P("mom", None, "phi", None, None),
            P(),
            P(),
            P(),
            P(),
            P(),
            P("mom"),
            P("phi", None, None),
        ),
        out_specs=P("mom", None, "phi", None, None),
        check_vma=False,
    )
```
